128 devices in a mesh: cfg: 2 (over x_hi), seq: 16 (over x_lo, y, core), fsdp: 4 (over z).
Axes of the slice: x: 4 (x_hi: 2, x_lo: 2; x = x_hi * 2 + x_lo), y: 4, z: 4, core: 2. Of those that a mesh axis runs over, the one named last changes fastest.
Arguments:
- q_video: bfloat16 [4, 2048, 3072], P('fsdp', 'seq'), may hold values from -30 to 30
- k_video: bfloat16 [4, 2048, 3072], P('fsdp', 'seq'), may hold values from -6 to 6
- v_video: bfloat16 [4, 2048, 3072], P('fsdp', 'seq'), may hold values from -6 to 6
- k_text: bfloat16 [2, 4, 256, 3072], P('cfg', 'fsdp', 'seq'), may hold values from -6 to 6
- v_text: bfloat16 [2, 4, 256, 3072], P('cfg', 'fsdp', 'seq'), may hold values from -6 to 6
- text_len: int32 [2, 4], P(None, 'fsdp'), may hold values from 64 to 256
- guide_index: int32 [4], P('fsdp'), may hold values from 0 to 6
- gate: float32 [4, 3072], P('fsdp'), may hold values from 0.1 to 1.9
- adjoint: bfloat16 [2, 4, 2048, 3072], P('cfg', 'fsdp', 'seq'), may hold values from -12 to 12
- w_out: bfloat16 [3072, 3072], P(('cfg', 'seq', 'fsdp')), may hold values from -0.109375 to 0.109375
Outputs:
- grad_q_video: bfloat16 [4, 2048, 3072], P('fsdp', 'seq')
- grad_k_video: bfloat16 [4, 2048, 3072], P('fsdp', 'seq')
- grad_v_video: bfloat16 [4, 2048, 3072], P('fsdp', 'seq')
- grad_k_text: bfloat16 [2, 4, 256, 3072], P('cfg', 'fsdp', 'seq')
- grad_v_text: bfloat16 [2, 4, 256, 3072], P('cfg', 'fsdp', 'seq')
The draws below stay inside these ranges and needn't reach their ends.
All inputs are finite; a program needn't handle non-finite values.
Results may differ from the reference program's by a relative error of at most 0.011.
Values may be sent and summed in bfloat16 or wider, within the bound.
No kernel may reach another device: no remote copies, remote signals or barrier semaphores. Data moves between devices by JAX's collectives and lax.ppermute only.
A program may use at most 128 MiB of HBM per device.

```python
import math
import jax
import jax.numpy as jnp
from jax import lax

D = 3072
HEADS = 24
HD = 128
TXT = 256
VID = 2048
CAND = 4


def draw_k_video(key, part):
    key = jax.random.fold_in(key, 11)
    result = jnp.clip(jax.random.normal(key, (CAND, VID, D), jnp.float32), -6.0, 6.0)
    return result.astype(jnp.bfloat16)


def draw_q_video(key, part):
    key = jax.random.fold_in(key, 23)
    result = jnp.clip(jax.random.normal(key, (CAND, VID, D), jnp.float32), -6.0, 6.0)
    return result.astype(jnp.bfloat16)


def plant(values, key, low, largest):
    index_at = [jax.random.randint(jax.random.fold_in(key, axis), (), 0, length) for axis, length in enumerate(values.shape)]
    widest = values.shape.index(max(values.shape))
    next_to = index_at[:widest] + [(index_at[widest] + 1) % values.shape[widest]] + index_at[widest + 1:]
    return values.at[tuple(index_at)].set(low).at[tuple(next_to)].set(largest)


def steps_of(key, dims, cuts, least, top_value):
    loudness, own = 1.0, jax.random.fold_in(key, 6)
    for axis_at, shards_of in cuts:
        draws = jnp.exp(jax.random.uniform(jax.random.fold_in(own, axis_at), (shards_of,), jnp.float32, least / len(cuts), top_value / len(cuts)))
        loudness = loudness * jnp.repeat(draws, dims[axis_at] // shards_of).reshape([-1 if axis == axis_at else 1 for axis in range(len(dims))])
    return loudness


def noise(stream_key, extent, spread, limit, cuts=(), held_as=jnp.bfloat16):
    level = steps_of(stream_key, extent, cuts, -0.22, 0.18) if cuts else 1.0
    drawn = jax.random.normal(stream_key, extent, jnp.float32) * spread * level
    return jnp.minimum(jnp.maximum(drawn, -limit), limit).astype(held_as)


def setup_inputs(seed: int = 0) -> dict:
    keys = jax.random.split(jax.random.key(seed), 11)
    q_video = draw_q_video(jax.random.fold_in(keys[10], 71), 0)
    k_video = draw_k_video(jax.random.fold_in(keys[10], 71), 0)
    v_video = noise(keys[2], (CAND, VID, D), 1.0, 6.0, ((0, 4), (1, 16)))
    k_text = noise(keys[3], (2, CAND, TXT, D), 1.0, 6.0, ((0, 2), (1, 4), (2, 16)))
    v_text = noise(keys[4], (2, CAND, TXT, D), 1.0, 6.0, ((0, 2), (1, 4), (2, 16)))
    text_len = plant(jax.random.randint(keys[5], (2, CAND), TXT // 4, TXT + 1), jax.random.fold_in(keys[5], 1), TXT // 4, TXT).astype(jnp.int32)
    guide_index = plant(jax.random.randint(keys[6], (CAND,), 0, 7), jax.random.fold_in(keys[6], 1), 0, 6).astype(jnp.int32)
    gate = jnp.clip(1.0 + 0.18 * jax.random.normal(keys[7], (CAND, D), jnp.float32), 0.1, 1.9)
    adjoint = noise(keys[8], (2, CAND, VID, D), 2.0, 12.0, ((0, 2), (1, 4), (2, 16)))
    w_out = noise(keys[9], (D, D), D ** -0.5, 0.109375, ((0, 128),))
    return dict(q_video=q_video, k_video=k_video, v_video=v_video, k_text=k_text, v_text=v_text, text_len=text_len, guide_index=guide_index, gate=gate, adjoint=adjoint, w_out=w_out)


def head_pass(queries, key_rows, value_rows, valid, adjoint_heads):
    factor = 1.0 / math.sqrt(queries.shape[-1])
    scores = jnp.dot(queries, key_rows.T, preferred_element_type=jnp.float32) * factor
    scores = jnp.where(valid[None, :], scores, -jnp.inf)
    row_max = lax.optimization_barrier(jnp.max(scores, axis=1, keepdims=True))
    exponent = jnp.exp(scores - row_max)
    weights = exponent / lax.optimization_barrier(jnp.sum(exponent, axis=1, keepdims=True))
    weights_low = weights.astype(jnp.bfloat16)
    attended = jnp.dot(weights_low, value_rows, preferred_element_type=jnp.float32)
    row_delta = lax.optimization_barrier(jnp.sum(adjoint_heads.astype(jnp.float32) * attended, axis=1, keepdims=True))
    grad_weights = jnp.dot(adjoint_heads, value_rows.T, preferred_element_type=jnp.float32)
    grad_scores = (weights * (grad_weights - row_delta)).astype(jnp.bfloat16)
    grad_query = (jnp.dot(grad_scores, key_rows, preferred_element_type=jnp.float32) * factor).astype(jnp.bfloat16)
    grad_keys = (jnp.dot(grad_scores.T, queries, preferred_element_type=jnp.float32) * factor).astype(jnp.bfloat16)
    grad_values = jnp.dot(weights_low.T, adjoint_heads, preferred_element_type=jnp.float32).astype(jnp.bfloat16)
    return (grad_query, grad_keys, grad_values)

def split_heads(matrix):
    return matrix.reshape(matrix.shape[0], HEADS, HD).transpose(1, 0, 2)

def merge_heads(stacked):
    return stacked.transpose(1, 0, 2).reshape(stacked.shape[1], HEADS * HD)

def pass_grads(query_rows, key_rows, value_rows, valid, adjoint_rows):

    def one_head(inputs):
        return head_pass(inputs[0], inputs[1], inputs[2], valid, inputs[3])
    results = lax.map(one_head, (split_heads(query_rows), split_heads(key_rows), split_heads(value_rows), split_heads(adjoint_rows)))
    return (merge_heads(results[0]), merge_heads(results[1]), merge_heads(results[2]))

def reference(q_video, k_video, v_video, k_text, v_text, text_len, guide_index, gate, adjoint, w_out):
    key_position = jnp.arange(VID + TXT, dtype=jnp.int32)
    query_out, key_out, value_out = ([], [], [])
    text_keys = [[], []]
    text_values = [[], []]
    for member in range(CAND):
        guidance = 1.5 + guide_index[member].astype(jnp.float32)
        query_total = jnp.zeros((VID, D), jnp.float32)
        key_total = jnp.zeros((VID, D), jnp.float32)
        value_total = jnp.zeros((VID, D), jnp.float32)
        for pass_index in range(2):
            pass_weight = guidance if pass_index == 0 else 1.0 - guidance
            scaled = (gate[member][None, :] * pass_weight * adjoint[pass_index, member].astype(jnp.float32)).astype(jnp.bfloat16)
            adjoint_out = jnp.dot(scaled, w_out.T, preferred_element_type=jnp.float32).astype(jnp.bfloat16)
            valid = key_position < VID + text_len[pass_index, member]
            key_rows = jnp.concatenate([k_video[member], k_text[pass_index, member]], axis=0)
            value_rows = jnp.concatenate([v_video[member], v_text[pass_index, member]], axis=0)
            grad_query, grad_keys, grad_values = pass_grads(q_video[member], key_rows, value_rows, valid, adjoint_out)
            query_total = query_total + grad_query.astype(jnp.float32)
            key_total = key_total + grad_keys[:VID].astype(jnp.float32)
            value_total = value_total + grad_values[:VID].astype(jnp.float32)
            text_keys[pass_index].append(grad_keys[VID:])
            text_values[pass_index].append(grad_values[VID:])
        query_out.append(query_total.astype(jnp.bfloat16))
        key_out.append(key_total.astype(jnp.bfloat16))
        value_out.append(value_total.astype(jnp.bfloat16))
    grad_k_text = jnp.stack([jnp.stack(text_keys[0]), jnp.stack(text_keys[1])])
    grad_v_text = jnp.stack([jnp.stack(text_values[0]), jnp.stack(text_values[1])])
    return (jnp.stack(query_out), jnp.stack(key_out), jnp.stack(value_out), grad_k_text, grad_v_text)
```

```python
import math

import jax
import jax.numpy as jnp
from jax import lax
from jax.experimental import pallas as pl
from jax.experimental.pallas import tpu as pltpu
from jax.sharding import PartitionSpec as P

HD = 128
TOK = 128
TT = 16
XW = 768
XH = 384
WROWS = 96
SCALE = 1.0 / math.sqrt(HD)
EXP2 = SCALE * math.log2(math.e)
VIDK = 2048
TXTK = 256


def dot(a, b, dims):
    return lax.dot_general(a, b, (dims, ((), ())), preferred_element_type=jnp.float32)


NT = ((1,), (1,))
NN = ((1,), (0,))
TN = ((0,), (0,))


def attn_kernel(bias_ref, q_ref, do_ref, k_ref, v_ref, dq_ref, dk_ref, dv_ref, dk_acc, dv_acc, ds_ref):
    step = pl.program_id(0)
    last = pl.num_programs(0) - 1
    q = q_ref[...]
    v_video = v_ref[:VIDK]
    s = dot(q, k_ref[:VIDK], NT)
    mv = jnp.max(s, axis=1, keepdims=True)
    e = jnp.exp2((s - mv) * EXP2)
    lv = jnp.sum(e, axis=1, keepdims=True)
    eb = e.astype(jnp.bfloat16)
    ov = dot(eb, v_video, NN)
    g = jnp.zeros(q.shape, jnp.float32)
    delta = jnp.zeros(lv.shape, jnp.float32)
    pbs = []
    for p in range(2):
        rows = slice(VIDK + p * TXTK, VIDK + (p + 1) * TXTK)
        vt = v_ref[rows]
        st = dot(q, k_ref[rows], NT) + bias_ref[p:p + 1, :]
        m = jnp.maximum(mv, jnp.max(st, axis=1, keepdims=True))
        a = jnp.exp2((mv - m) * EXP2)
        et = jnp.exp2((st - m) * EXP2)
        inv = 1.0 / (a * lv + jnp.sum(et, axis=1, keepdims=True))
        w = a * inv
        pt = et * inv
        ptb = pt.astype(jnp.bfloat16)
        do = do_ref[:, p].reshape(q.shape)
        do32 = do.astype(jnp.float32)
        o = w * ov + dot(ptb, vt, NN)
        dl = jnp.sum(do32 * o, axis=1, keepdims=True)
        g = g + w * do32
        delta = delta + w * dl
        dst = pt * (dot(do, vt, NT) - dl)
        ds_ref[:, rows] = dst.astype(jnp.bfloat16)
        pbs.append((ptb, do))
    gb = g.astype(jnp.bfloat16)
    delta = delta + jnp.sum((gb.astype(jnp.float32) - g) * ov, axis=1, keepdims=True) / lv
    dp = dot(gb, v_video, NT)
    ds_ref[:, :VIDK] = (e * (dp - delta)).astype(jnp.bfloat16)
    ds = ds_ref[...]
    dq_ref[...] = (dot(ds, k_ref[...], NN) * SCALE).astype(jnp.bfloat16)
    dk = dot(ds, q, TN)
    dv = jnp.concatenate([dot(eb, gb, TN)] + [dot(ptb, do, TN) for ptb, do in pbs], axis=0)

    @pl.when(step == 0)
    def _():
        dk_acc[...] = dk
        dv_acc[...] = dv

    @pl.when(step > 0)
    def _():
        dk_acc[...] += dk
        dv_acc[...] += dv

    @pl.when(step == last)
    def _():
        dk_ref[...] = (dk_acc[...] * SCALE).astype(jnp.bfloat16)
        dv_ref[...] = dv_acc[...].astype(jnp.bfloat16)


def attention(bias, q, do, k, v, block=256):
    nq = q.shape[0]
    per = do.shape[2]
    nk = k.shape[0]
    full = lambda *shape: pl.BlockSpec(shape, lambda i: (0,) * len(shape))
    return pl.pallas_call(
        attn_kernel,
        grid=(nq // block,),
        in_specs=[
            full(2, TXTK),
            pl.BlockSpec((block, HD), lambda i: (i, 0)),
            pl.BlockSpec((block // per, 2, per, HD), lambda i: (i, 0, 0, 0)),
            full(nk, HD),
            full(nk, HD),
        ],
        out_specs=[
            pl.BlockSpec((block, HD), lambda i: (i, 0)),
            full(nk, HD),
            full(nk, HD),
        ],
        out_shape=[
            jax.ShapeDtypeStruct((nq, HD), jnp.bfloat16),
            jax.ShapeDtypeStruct((nk, HD), jnp.bfloat16),
            jax.ShapeDtypeStruct((nk, HD), jnp.bfloat16),
        ],
        scratch_shapes=[
            pltpu.VMEM((nk, HD), jnp.float32),
            pltpu.VMEM((nk, HD), jnp.float32),
            pltpu.VMEM((block, nk), jnp.bfloat16),
        ],
        compiler_params=pltpu.CompilerParams(vmem_limit_bytes=48 * 1024 * 1024),
        cost_estimate=pl.CostEstimate(flops=12 * nq * nk * HD, bytes_accessed=4 * nk * HD * 2, transcendentals=nq * nk),
    )(bias, q, do, k, v)


def swap(a, axis):
    return lax.ppermute(a, axis, [(0, 1), (1, 0)])


def x_swap(a, r):
    if r == 1:
        return swap(a, "xlo")
    if r == 2:
        return swap(a, "cfg")
    return lax.ppermute(a, ("cfg", "xlo"), [(i, 3 - i) for i in range(4)])


def y_swap(a, r):
    return lax.ppermute(a, "y", [(i, i ^ r) for i in range(4)])


def cols(a, start, width):
    return lax.dynamic_slice_in_dim(a, start, width, axis=a.ndim - 1)


def own_head(a, y):
    return cols(a, y * HD, HD)


def shared_head(a, y):
    return cols(a, (4 + y // 2) * HD, HD)


def half_rows(a, y):
    return lax.dynamic_slice_in_dim(a, (y % 2) * (TOK // 2), TOK // 2, axis=a.ndim - 2)


def flat(*parts):
    return jnp.concatenate([part.reshape(-1, HD) for part in parts], axis=0)


def project_kernel(place_ref, *refs):
    y, c = place_ref[0], place_ref[1]
    w_refs, a_refs = refs[:8], refs[8:13]
    out_ref, w_all, a_all, sems = refs[13:]
    copies = []
    for other in range(2):
        for r in range(4):
            row = pl.multiple_of(((y ^ r) * 2 + (c ^ other)) * WROWS, WROWS)
            copies.append((w_refs[other * 4 + r], w_all.at[pl.ds(row, WROWS)]))
    row = 0
    for a_ref in a_refs:
        count = a_ref.shape[0]
        copies.append((a_ref, a_all.at[pl.ds(row, count)]))
        row += count
    started = [
        pltpu.make_async_copy(src, dst, sems.at[i]) for i, (src, dst) in enumerate(copies)
    ]
    for copy in started:
        copy.start()
    for copy in started:
        copy.wait()
    out_ref[...] = dot(a_all[...], w_all[...], NT).astype(jnp.bfloat16)


def project(place, w_pieces, a_pieces):
    rows = sum(a.shape[0] for a in a_pieces)
    width = w_pieces[0].shape[1]
    count = len(w_pieces) * w_pieces[0].shape[0]
    pieces = len(w_pieces) + len(a_pieces)
    return pl.pallas_call(
        project_kernel,
        in_specs=[pl.BlockSpec(memory_space=pltpu.SMEM)]
        + [pl.BlockSpec(memory_space=pl.ANY)] * pieces,
        out_specs=pl.BlockSpec(memory_space=pltpu.VMEM),
        out_shape=jax.ShapeDtypeStruct((rows, count), jnp.bfloat16),
        scratch_shapes=[
            pltpu.VMEM((count, width), jnp.bfloat16),
            pltpu.VMEM((rows, width), jnp.bfloat16),
            pltpu.SemaphoreType.DMA((pieces,)),
        ],
        compiler_params=pltpu.CompilerParams(vmem_limit_bytes=40 * 1024 * 1024),
        cost_estimate=pl.CostEstimate(
            flops=2 * rows * count * width,
            bytes_accessed=2 * (rows + count) * width + 2 * rows * count,
            transcendentals=0,
        ),
    )(place, *w_pieces, *a_pieces)


def local(q_video, k_video, v_video, k_text, v_text, text_len, guide_index, gate, adjoint, w_out):
    h = lax.axis_index("cfg")
    l = lax.axis_index("xlo")
    y = lax.axis_index("y")
    c = lax.axis_index("core")
    x = 2 * h + l
    q, k, v = q_video[0], k_video[0], v_video[0]
    kt, vt = k_text[0, 0], v_text[0, 0]

    guidance = 1.5 + guide_index[0].astype(jnp.float32)
    pass_weight = jnp.where(h == 0, guidance, 1.0 - guidance)
    scaled = (gate[0][None, :] * pass_weight * adjoint[0, 0].astype(jnp.float32)).astype(
        jnp.bfloat16
    )
    scaled1 = x_swap(scaled, 1)
    scaled3 = x_swap(scaled, 3)
    half = TOK // 2
    scaled2a = x_swap(scaled3[:half], 1)
    scaled2b = x_swap(scaled1[half:], 3)

    w_z = lax.all_gather(w_out, "fsdp", axis=0, tiled=True)
    w_own = [w_z] + [y_swap(w_z, r) for r in (1, 2, 3)]
    w_other = [swap(piece, "core") for piece in w_own]

    def text_rows(r):
        parts = [cols(a, (x ^ r) * XW, XW) for a in (kt, vt)]
        return [part[:, i * XH : (i + 1) * XH] for part in parts for i in range(2)]

    def video_rows(r, place):
        return [cols(a, (x ^ r) * XW + place * XH, XH) for a in (q, k, v)]

    got1 = x_swap(jnp.concatenate(video_rows(1, 0) + text_rows(1), axis=0), 1)
    got3 = x_swap(jnp.concatenate(video_rows(3, 1) + text_rows(3), axis=0), 3)
    got2 = x_swap(jnp.concatenate(text_rows(2), axis=0), 2)

    def video_at(i):
        own = cols((q, k, v)[i], x * XW, XW)
        rows = slice(i * TOK, (i + 1) * TOK)
        other = jnp.concatenate([got1[rows], got3[rows]], axis=1)
        return jnp.stack([own, other])

    q6, k6, v6 = video_at(0), video_at(1), video_at(2)

    def text_at(i):
        own = cols((kt, vt)[i], x * XW, XW)
        parts = [own]
        for got, start in ((got1, 3 * TOK), (got2, 0), (got3, 3 * TOK)):
            row = start + 2 * i * TT
            parts.append(jnp.concatenate([got[row : row + TT], got[row + TT : row + 2 * TT]], axis=1))
        return jnp.stack(parts)

    kt6, vt6 = text_at(0), text_at(1)

    def message(yd):
        return flat(
            own_head(k6, yd),
            own_head(v6, yd),
            own_head(kt6, yd),
            own_head(vt6, yd),
            shared_head(k6, yd),
            shared_head(v6, yd),
            shared_head(kt6, yd),
            shared_head(vt6, yd),
            own_head(q6, yd),
            half_rows(shared_head(q6, yd), yd),
        )

    arrived = jnp.stack([message(y)] + [y_swap(message(y ^ r), r) for r in (1, 2, 3)])
    kv_rows = 2 * (4 * TOK + 8 * TT)
    other_kv = swap(arrived[:, :kv_rows], "core")
    both = jnp.stack([arrived[:, :kv_rows], other_kv])

    def keys_values(head):
        start = head * (kv_rows // 2)
        out = []
        for i in range(2):
            video = both[:, :, start + i * 2 * TOK : start + (i + 1) * 2 * TOK]
            row = start + 4 * TOK + i * 4 * TT
            text = [both[:, :, row + p * 2 * TT : row + (p + 1) * 2 * TT] for p in range(2)]
            out.append(flat(video, *text))
        return out

    k_a, v_a = keys_values(0)
    k_b, v_b = keys_values(1)
    q_a = arrived[:, kv_rows : kv_rows + 2 * TOK].reshape(-1, HD)
    q_b = arrived[:, kv_rows + 2 * TOK :].reshape(-1, HD)

    lc = jnp.arange(2, dtype=jnp.int32)
    at_core = (c ^ lc)[:, None, None, None]
    at_y = (y ^ jnp.arange(4, dtype=jnp.int32))[None, :, None, None]
    at_l = (l ^ lc)[None, None, :, None]
    position = ((at_l * 4 + at_y) * 2 + at_core) * TT + jnp.arange(TT, dtype=jnp.int32)
    position = position.reshape(1, -1)
    lens = jnp.where(h == 0, text_len[:, 0], text_len[::-1, 0])
    bias = jnp.where(position < lens[:, None], 0.0, -jnp.inf).astype(jnp.float32)

    place = jnp.stack([y, c]).astype(jnp.int32)
    adj = project(place, w_own + w_other, [scaled, scaled1, scaled2a, scaled2b, scaled3])
    adj = adj.reshape(4, TOK, XW)

    def adj_b(yd):
        return half_rows(shared_head(adj, yd), yd).reshape(2, TOK, HD)

    def adj_a(yd):
        return own_head(adj, yd).reshape(2, 2 * TOK, HD)

    do_b = jnp.stack([adj_b(y)] + [y_swap(adj_b(y ^ r), r) for r in (1, 2, 3)])
    do_a = jnp.stack([adj_a(y)] + [y_swap(adj_a(y ^ r), r) for r in (1, 2, 3)])

    dq_b, dk_b, dv_b = attention(bias, q_b, do_b, k_b, v_b)
    dq_a, dk_a, dv_a = attention(bias, q_a, do_a, k_a, v_a)

    def split_core(a):
        video = a[:VIDK].reshape(2, 4, 2 * TOK, HD)
        text = a[VIDK:].reshape(2, 2, 4, 2 * TT, HD)
        text = jnp.moveaxis(text, 0, 2)
        return jnp.concatenate([video, text.reshape(2, 4, 4 * TT, HD)], axis=2)

    pieces = [split_core(a) for a in (dk_a, dv_a, dk_b, dv_b)]
    sent = jnp.stack([piece[1] for piece in pieces])
    kept = jnp.stack([piece[0] for piece in pieces])
    came = swap(sent, "core")
    summed = (kept.astype(jnp.float32) + came.astype(jnp.float32)).astype(jnp.bfloat16)
    dq_a = dq_a.reshape(4, 2 * TOK, HD)
    dq_b = dq_b.reshape(4, TOK, HD)

    def back(r):
        return flat(summed[:, r], dq_a[r], dq_b[r])

    returned = jnp.stack([back(0)] + [y_swap(back(r), r) for r in (1, 2, 3)])
    rows = 2 * TOK + 4 * TT

    def order_heads(head_a, head_b):
        parts = [lax.dynamic_index_in_dim(head_a, y ^ j, 0, False) for j in range(4)]
        parts += [lax.dynamic_index_in_dim(head_b, (y // 2) ^ j, 0, False) for j in range(2)]
        return jnp.concatenate(parts, axis=-1)

    def key_value(i):
        head_a = returned[:, i * rows : (i + 1) * rows]
        head_b = returned[:, (2 + i) * rows : (3 + i) * rows].astype(jnp.float32)
        head_b = (head_b[0::2] + head_b[1::2]).astype(jnp.bfloat16)
        return order_heads(head_a, head_b)

    def query():
        head_a = returned[:, 4 * rows : 4 * rows + 2 * TOK]
        head_b = returned[:, 4 * rows + 2 * TOK :].reshape(2, 2, 2, TOK // 2, HD)
        first = lax.dynamic_index_in_dim(head_b, y % 2, 1, False)
        second = lax.dynamic_index_in_dim(head_b, 1 - y % 2, 1, False)
        head_b = jnp.stack([first, second], axis=2).reshape(2, 2 * TOK, HD)
        return order_heads(head_a, head_b)

    dq6 = query()
    dk6, dv6 = key_value(0), key_value(1)
    own_rows = [dq6[:TOK], dk6[:TOK], dv6[:TOK]]
    far_rows = [dq6[TOK:], dk6[TOK : 2 * TOK], dv6[TOK : 2 * TOK]]

    def text_of(r):
        return [a[2 * TOK + r * TT : 2 * TOK + (r + 1) * TT] for a in (dk6, dv6)]

    final = jnp.stack(
        [
            jnp.concatenate(own_rows + text_of(0), axis=0),
            x_swap(jnp.concatenate(far_rows + text_of(1), axis=0), 1),
            x_swap(jnp.concatenate(own_rows + text_of(2), axis=0), 2),
            x_swap(jnp.concatenate(far_rows + text_of(3), axis=0), 3),
        ]
    )

    def whole(start, count):
        part = final[:, start : start + count]
        return jnp.concatenate(
            [lax.dynamic_index_in_dim(part, x ^ j, 0, False) for j in range(4)], axis=1
        )

    return (
        whole(0, TOK)[None],
        whole(TOK, TOK)[None],
        whole(2 * TOK, TOK)[None],
        whole(3 * TOK, TT)[None, None],
        whole(3 * TOK + TT, TT)[None, None],
    )


def solution(mesh):
    devices = mesh.devices
    fine = jax.sharding.Mesh(
        devices.reshape(2, 2, 4, 2, devices.shape[-1]), ("cfg", "xlo", "y", "core", "fsdp")
    )
    seq = ("xlo", "y", "core")
    video = P("fsdp", seq, None)
    per_pass = P("cfg", "fsdp", seq, None)
    placed = (
        video,
        video,
        video,
        per_pass,
        per_pass,
        P(None, "fsdp"),
        P("fsdp"),
        P("fsdp", None),
        per_pass,
        P(("cfg",) + seq + ("fsdp",), None),
    )
    return jax.shard_map(
        local,
        mesh=fine,
        in_specs=placed,
        out_specs=(video, video, video, per_pass, per_pass),
        check_vma=False,
    )
```

```python
import math

import jax
import jax.numpy as jnp
from jax import lax
from jax.experimental import pallas as pl
from jax.experimental.pallas import tpu as pltpu
from jax.sharding import PartitionSpec as P

HD = 128
TOK = 128
TT = 16
XH = 6
XW = XH * HD
WROWS = 96
SCALE = 1.0 / math.sqrt(HD)
EXP2 = SCALE * math.log2(math.e)
VIDK = 2048
TXTK = 256
BLOCK = 256

NT = ((1,), (1,))
NN = ((1,), (0,))
TN = ((0,), (0,))

K_A, V_A, K_B, V_B = 0, 2 * TOK, 4 * TOK, 6 * TOK
TK_A, TV_A, TK_B, TV_B = (8 * TOK + i * 4 * TT for i in range(4))
Q_A = 8 * TOK + 16 * TT
Q_B = Q_A + 2 * TOK
MSG = Q_B + TOK
OWN = 3 * TOK + 2 * TT
NEAR = 3 * TOK // 2 + 2 * TT
BACK_KV = 4 * TOK + 8 * TT


def dot(a, b, dims):
    return lax.dot_general(a, b, (dims, ((), ())), preferred_element_type=jnp.float32)


def vmem_specs(count):
    return [pl.BlockSpec(memory_space=pltpu.VMEM)] * count


SMEM = pl.BlockSpec(memory_space=pltpu.SMEM)
MIB = 1024 * 1024


def params(mib):
    return pltpu.CompilerParams(vmem_limit_bytes=mib * MIB)


COST = pl.CostEstimate(flops=0, bytes_accessed=0, transcendentals=0)


def whole(a):
    shape = a.shape
    return pl.BlockSpec(shape, lambda *_: (0,) * len(shape))


def lanes(start, count):
    return pl.ds(pl.multiple_of(start, HD), count)


def run_copies(copies, sems):
    started = [pltpu.make_async_copy(src, dst, sems.at[i]) for i, (src, dst) in enumerate(copies)]
    for copy in started:
        copy.start()
    for copy in started:
        copy.wait()


def swap(a, axis):
    return lax.ppermute(a, axis, [(0, 1), (1, 0)])


def x_swap(a, r):
    if r == 1:
        return swap(a, "xlo")
    if r == 2:
        return swap(a, "cfg")
    return lax.ppermute(a, ("cfg", "xlo"), [(i, 3 - i) for i in range(4)])


def ring_swap(a, axis, r):
    return lax.ppermute(a, axis, [(i, i ^ r) for i in range(4)])


def bf16(*shape):
    return jax.ShapeDtypeStruct(shape, jnp.bfloat16)


def cut_x_kernel(at_ref, *refs):
    del at_ref
    blocks, outs = refs[:17], refs[17:]
    for out, first, count in zip(outs, (0, 5, 10, 15), (5, 5, 5, 2)):
        row = 0
        for block in blocks[first : first + count]:
            out[row : row + block.shape[0]] = block[...]
            row += block.shape[0]


def cut_x(at, q, k, v, kt, vt):
    half = TOK // 2

    def block(rows, r, index):
        return pl.BlockSpec((rows, XW), lambda i, at_ref: (index, at_ref[0] ^ r))

    def same(a):
        return pl.BlockSpec(a.shape, lambda i, at_ref: (0, 0))

    specs, arrays = [], []
    for rows, r, index in ((TOK, 0, 0), (half, 1, 0), (half, 3, 1)):
        specs += [block(rows, r, index)] * 3 + [block(TT, r, 0)] * 2
        arrays += [q, k, v, kt, vt]
    specs += [block(TT, 2, 0)] * 2
    arrays += [kt, vt]
    shapes = [bf16(OWN, XW), bf16(NEAR, XW), bf16(NEAR, XW), bf16(2 * TT, XW)]
    return pl.pallas_call(
        cut_x_kernel,
        grid_spec=pltpu.PrefetchScalarGridSpec(
            num_scalar_prefetch=1,
            grid=(1,),
            in_specs=specs,
            out_specs=[same(a) for a in shapes],
        ),
        out_shape=shapes,
        compiler_params=params(60),
        cost_estimate=COST,
    )(at, *arrays)


def cut_y_kernel(at_ref, own, got1, got2, got3, *outs):
    y = at_ref[1]
    half = TOK // 2
    quarter = TOK // 4
    for r, out in enumerate(outs):
        yd = y ^ r
        head_a = lanes(yd * HD, HD)
        head_b = lanes((4 + yd // 2) * HD, HD)
        for row, tensor, head in (
            (K_A, 1, head_a),
            (V_A, 2, head_a),
            (K_B, 1, head_b),
            (V_B, 2, head_b),
            (Q_A, 0, head_a),
        ):
            out[row : row + TOK] = own[tensor * TOK : (tensor + 1) * TOK, head]
            rows = slice(tensor * half, (tensor + 1) * half)
            out[row + TOK : row + TOK + half] = got1[rows, head]
            out[row + TOK + half : row + 2 * TOK] = got3[rows, head]
        for row, tensor, head in (
            (TK_A, 0, head_a),
            (TV_A, 1, head_a),
            (TK_B, 0, head_b),
            (TV_B, 1, head_b),
        ):
            for s, (src, first) in enumerate(
                ((own, 3 * TOK), (got1, 3 * half), (got2, 0), (got3, 3 * half))
            ):
                start = first + tensor * TT
                out[row + s * TT : row + (s + 1) * TT] = src[start : start + TT, head]
        skip = (yd % 2) * quarter
        for i, (src, first) in enumerate(((own, 0), (own, half), (got1, 0), (got3, 0))):
            rows = pl.ds(pl.multiple_of(first + skip, quarter), quarter)
            out[Q_B + i * quarter : Q_B + (i + 1) * quarter] = src[rows, head_b]


def cut_y(at, own, got1, got2, got3):
    arrays = (own, got1, got2, got3)
    shapes = [bf16(MSG, HD)] * 4
    return pl.pallas_call(
        cut_y_kernel,
        in_specs=[SMEM] + [whole(a) for a in arrays],
        out_specs=[whole(a) for a in shapes],
        out_shape=shapes,
        compiler_params=params(8),
        cost_estimate=COST,
    )(at, *arrays)


def project_kernel(at_ref, *refs):
    y, c = at_ref[1], at_ref[2]
    w_refs, a_refs, outs = refs[:8], refs[8:13], refs[13:17]
    w_all, a_all, out = refs[17:]
    for i, ref in enumerate(w_refs):
        row = pl.multiple_of(((y ^ (i % 4)) * 2 + (c ^ (i // 4))) * WROWS, WROWS)
        w_all[pl.ds(row, WROWS)] = ref[...]
    row = 0
    for ref in a_refs:
        a_all[row : row + ref.shape[0]] = ref[...]
        row += ref.shape[0]
    out[...] = dot(a_all[...], w_all[...], NT).astype(jnp.bfloat16)
    quarter = TOK // 4
    for r in range(4):
        yd = y ^ r
        outs[r][: 4 * TOK] = out[:, lanes(yd * HD, HD)]
        head_b = lanes((4 + yd // 2) * HD, HD)
        skip = (yd % 2) * quarter
        for i in range(8):
            rows = pl.ds(pl.multiple_of(i * 2 * quarter + skip, quarter), quarter)
            outs[r][4 * TOK + i * quarter : 4 * TOK + (i + 1) * quarter] = out[rows, head_b]


def project(at, weights, adjoints):
    width = weights[0].shape[1]
    rows = 4 * TOK
    return pl.pallas_call(
        project_kernel,
        in_specs=[SMEM] + vmem_specs(13),
        out_specs=vmem_specs(4),
        out_shape=[bf16(rows + rows // 2, HD)] * 4,
        scratch_shapes=[
            pltpu.VMEM((XW, width), jnp.bfloat16),
            pltpu.VMEM((rows, width), jnp.bfloat16),
            pltpu.VMEM((rows, XW), jnp.bfloat16),
        ],
        compiler_params=params(16),
        cost_estimate=COST,
    )(at, *weights, *adjoints)


def forward_kernel(bias_ref, *refs):
    msgs = refs[:8]
    e_ref, p_ref, o_ref, w_ref, k_all, v_all, q_ref, q_all = refs[8:]
    step = pl.program_id(0)
    run = 2 * TT

    @pl.when(step == 0)
    def _():
        for head, (k_at, v_at, tk_at, tv_at) in enumerate(
            ((K_A, V_A, TK_A, TV_A), (K_B, V_B, TK_B, TV_B))
        ):
            for i, msg in enumerate(msgs):
                video = slice(i * 2 * TOK, (i + 1) * 2 * TOK)
                k_all[head, video] = msg[k_at : k_at + 2 * TOK]
                v_all[head, video] = msg[v_at : v_at + 2 * TOK]
                for p in range(2):
                    row = VIDK + p * TXTK + i * run
                    k_all[head, row : row + run] = msg[tk_at + p * run : tk_at + (p + 1) * run]
                    v_all[head, row : row + run] = msg[tv_at + p * run : tv_at + (p + 1) * run]
        for r in range(4):
            q_all[r * 2 * TOK : (r + 1) * 2 * TOK] = msgs[r][Q_A : Q_A + 2 * TOK]
            q_all[8 * TOK + r * TOK : 8 * TOK + (r + 1) * TOK] = msgs[r][Q_B : Q_B + TOK]

    head = step // 4
    q = q_all[pl.ds(pl.multiple_of(step * BLOCK, BLOCK), BLOCK)]
    q_ref[...] = q
    s = dot(q, k_all[head, :VIDK], NT)
    mv = jnp.max(s, axis=1, keepdims=True)
    e = jnp.exp2((s - mv) * EXP2)
    lv = jnp.sum(e, axis=1, keepdims=True)
    eb = e.astype(jnp.bfloat16)
    e_ref[...] = eb
    ov = dot(eb, v_all[head, :VIDK], NN)
    o_ref[2] = ov / lv
    for p in range(2):
        text = slice(VIDK + p * TXTK, VIDK + (p + 1) * TXTK)
        st = dot(q, k_all[head, text], NT) + bias_ref[p : p + 1, :]
        m = jnp.maximum(mv, jnp.max(st, axis=1, keepdims=True))
        a = jnp.exp2((mv - m) * EXP2)
        et = jnp.exp2((st - m) * EXP2)
        inv = 1.0 / (a * lv + jnp.sum(et, axis=1, keepdims=True))
        w = a * inv
        pt = (et * inv).astype(jnp.bfloat16)
        p_ref[p] = pt
        w_ref[p] = jnp.broadcast_to(w, w_ref.shape[1:])
        o_ref[p] = w * ov + dot(pt, v_all[head, text], NN)


def attention_forward(bias, own, other):
    keys = VIDK + 2 * TXTK
    rows = 12 * TOK
    arrays = (bias, *own, *other)
    heads = bf16(2, keys, HD)

    def stacked(count, width):
        return pl.BlockSpec((count, BLOCK, width), lambda i: (0, i, 0))

    return pl.pallas_call(
        forward_kernel,
        grid=(rows // BLOCK,),
        in_specs=[whole(a) for a in arrays],
        out_specs=[
            pl.BlockSpec((BLOCK, VIDK), lambda i: (i, 0)),
            stacked(2, TXTK),
            stacked(3, HD),
            stacked(2, HD),
            whole(heads),
            whole(heads),
            pl.BlockSpec((BLOCK, HD), lambda i: (i, 0)),
        ],
        out_shape=[
            bf16(rows, VIDK),
            bf16(2, rows, TXTK),
            jax.ShapeDtypeStruct((3, rows, HD), jnp.float32),
            jax.ShapeDtypeStruct((2, rows, HD), jnp.float32),
            heads,
            heads,
            bf16(rows, HD),
        ],
        scratch_shapes=[pltpu.VMEM((rows, HD), jnp.bfloat16)],
        compiler_params=params(24),
        cost_estimate=COST,
    )(*arrays)


def backward_kernel(shape, *refs):
    parts, first, final, count, do_at = shape
    e_ref, p_ref, o_ref, w_ref, q_ref, k_ref, v_ref = refs[:7]
    dos, refs = refs[7 : 7 + parts], refs[7 + parts :]
    if not first:
        dk_in, dv_in, refs = refs[0], refs[1], refs[2:]
    out0, out1, dqs = refs[0], refs[1], refs[2 : 2 + parts]
    ds_all, dk_acc, dv_acc = refs[2 + parts :]
    step = pl.program_id(0)
    last = pl.num_programs(0) - 1
    per_step = BLOCK // count
    run = 2 * TT

    @pl.when(step == 0)
    def _():
        dk_acc[...] = jnp.zeros_like(dk_acc) if first else dk_in[...]
        dv_acc[...] = jnp.zeros_like(dv_acc) if first else dv_in[...]

    def adjoint(p):
        rows = slice(do_at + p * count, do_at + (p + 1) * count)
        value = jnp.concatenate([ref[rows] for ref in dos[:per_step]], axis=0)
        for i in range(1, parts // per_step):
            group = dos[i * per_step : (i + 1) * per_step]
            other = jnp.concatenate([ref[rows] for ref in group], axis=0)
            value = jnp.where(step == i, other, value)
        return value

    q = q_ref[...]
    v_video = v_ref[:VIDK]
    g = jnp.zeros(q.shape, jnp.float32)
    delta = jnp.zeros((BLOCK, 1), jnp.float32)
    for p in range(2):
        text = slice(VIDK + p * TXTK, VIDK + (p + 1) * TXTK)
        do = adjoint(p)
        do32 = do.astype(jnp.float32)
        w = w_ref[p]
        row_delta = jnp.sum(do32 * o_ref[p], axis=1, keepdims=True)
        g = g + w * do32
        delta = delta + w[:, :1] * row_delta
        pt = p_ref[p]
        ds_text = pt.astype(jnp.float32) * (dot(do, v_ref[text], NT) - row_delta)
        ds_all[:, text] = ds_text.astype(jnp.bfloat16)
        dv_acc[text] += dot(pt, do, TN)
    gb = g.astype(jnp.bfloat16)
    delta = delta + jnp.sum((gb.astype(jnp.float32) - g) * o_ref[2], axis=1, keepdims=True)
    e = e_ref[...]
    ds_video = e.astype(jnp.float32) * (dot(gb, v_video, NT) - delta)
    ds_all[:, :VIDK] = ds_video.astype(jnp.bfloat16)
    dv_acc[:VIDK] += dot(e, gb, TN)
    ds = ds_all[...]
    dk_acc[...] += dot(ds, q, TN)
    dq = (dot(ds, k_ref[...], NN) * SCALE).astype(jnp.bfloat16)
    for r in range(parts):

        @pl.when(step == r // per_step)
        def _():
            start = (r % per_step) * count
            dqs[r][...] = dq[start : start + count]

    @pl.when(step == last)
    def _():
        if not final:
            out0[...] = dk_acc[...]
            out1[...] = dv_acc[...]
            return
        for i in range(8):
            out = (out0, out1)[i // 4].at[i % 4]
            for j, acc, factor in ((0, dk_acc, SCALE), (1, dv_acc, 1.0)):
                video = acc[i * 2 * TOK : (i + 1) * 2 * TOK] * factor
                out[j * 2 * TOK : (j + 1) * 2 * TOK] = video.astype(jnp.bfloat16)
                for p in range(2):
                    src = VIDK + p * TXTK + i * run
                    dst = 4 * TOK + j * 2 * run + p * run
                    out[dst : dst + run] = (acc[src : src + run] * factor).astype(jnp.bfloat16)


def attention_backward(stored, dos, shared, start=0, sums=None, final=True):
    e, p, o, w, k, v, q = stored
    parts = len(dos)
    count = TOK if shared else 2 * TOK
    do_at = 4 * TOK if shared else 0
    steps = parts * count // BLOCK
    head = 1 if shared else 0
    skip = (8 * TOK if shared else 0) // BLOCK + start * count // BLOCK
    keys = VIDK + 2 * TXTK
    shape = (parts, sums is None, final, count, do_at)

    def kernel(*refs):
        backward_kernel(shape, *refs)

    def stacked(depth, width):
        return pl.BlockSpec((depth, BLOCK, width), lambda i: (0, i + skip, 0))

    def rows_of(width):
        return pl.BlockSpec((BLOCK, width), lambda i: (i + skip, 0))

    keys_of = pl.BlockSpec((None, keys, HD), lambda i: (head, 0, 0))
    sum_shape = jax.ShapeDtypeStruct((keys, HD), jnp.float32)
    sums = [] if sums is None else list(sums)
    results = pl.pallas_call(
        kernel,
        grid=(steps,),
        in_specs=[rows_of(VIDK), stacked(2, TXTK), stacked(3, HD), stacked(2, HD), rows_of(HD)]
        + [keys_of, keys_of]
        + vmem_specs(parts + len(sums)),
        out_specs=vmem_specs(2 + parts),
        out_shape=([bf16(4, BACK_KV, HD)] * 2 if final else [sum_shape] * 2)
        + [bf16(count, HD)] * parts,
        scratch_shapes=[
            pltpu.VMEM((BLOCK, keys), jnp.bfloat16),
            pltpu.VMEM((keys, HD), jnp.float32),
            pltpu.VMEM((keys, HD), jnp.float32),
        ],
        compiler_params=params(18),
        cost_estimate=COST,
    )(e, p, o, w, q, k, v, *dos, *sums)
    return results[0], results[1], results[2:]


def add_cores_kernel(kept, came, *refs):
    dqs, outs = refs[:4], refs[4:]
    for r, out in enumerate(outs):
        total = kept[r].astype(jnp.float32) + came[r].astype(jnp.float32)
        out[:BACK_KV] = total.astype(jnp.bfloat16)
        out[BACK_KV:] = dqs[r][...]


def add_cores(kept, came, dqs):
    count = dqs[0].shape[0]
    return pl.pallas_call(
        add_cores_kernel,
        in_specs=vmem_specs(6),
        out_specs=vmem_specs(4),
        out_shape=[bf16(BACK_KV + count, HD)] * 4,
        compiler_params=params(8),
        cost_estimate=COST,
    )(kept, came, *dqs)


def merge_y_kernel(shared, at_ref, *refs):
    y = at_ref[1]
    got, outs = refs[:4], refs[4:]
    quarter = TOK // 4

    def put(out, row, head, value):
        out[row : row + value.shape[0], head] = value

    def part(r, rows):
        if not shared:
            return got[r][rows]
        total = got[r][rows].astype(jnp.float32) + got[r + 1][rows].astype(jnp.float32)
        return total.astype(jnp.bfloat16)

    for r in (0, 2) if shared else range(4):
        head = lanes(((y // 2) ^ (r // 2)) * HD, HD) if shared else lanes((y ^ r) * HD, HD)
        for j in range(2):
            for par in range(2):
                first = (2 * j + par) * TOK
                value = part(r, slice(first, first + TOK))
                for s in (par, par + 2):
                    if (s, par) in ((0, 0), (2, 0), (1, 1), (3, 1)):
                        put(outs[s], (1 + j) * TOK, head, value)
            for s in range(4):
                first = 4 * TOK + j * 4 * TT + s * TT
                value = part(r, slice(first, first + TT))
                put(outs[s], 3 * TOK + j * TT, head, value)
        for par in range(2):
            if not shared:
                value = got[r][BACK_KV + par * TOK : BACK_KV + (par + 1) * TOK]
                for s in (par, par + 2):
                    put(outs[s], 0, head, value)
                continue
            for rr in (r, r + 1):
                skip = ((y ^ rr) % 2) * quarter
                for i in range(2):
                    first = BACK_KV + par * 2 * quarter + i * quarter
                    value = got[rr][first : first + quarter]
                    rows = pl.ds(pl.multiple_of(i * 2 * quarter + skip, quarter), quarter)
                    for s in (par, par + 2):
                        outs[s][rows, head] = value


def merge_y(at, got, shared):
    width = (2 if shared else 4) * HD

    def kernel(*refs):
        merge_y_kernel(shared, *refs)

    return pl.pallas_call(
        kernel,
        in_specs=[SMEM] + vmem_specs(4),
        out_specs=vmem_specs(4),
        out_shape=[bf16(3 * TOK + 2 * TT, width)] * 4,
        compiler_params=params(8),
        cost_estimate=COST,
    )(at, *got)


def merge_x_kernel(at_ref, *refs):
    x = at_ref[0]
    parts_a, parts_b, outs = refs[:4], refs[4:8], refs[8:13]
    for r in range(4):
        for part, first in ((parts_a[r], 0), (parts_b[r], 4 * HD)):
            col = lanes((x ^ r) * XW + first, part.shape[1])
            row = 0
            for out in outs:
                count = out.shape[0]
                out[:, col] = part[row : row + count]
                row += count


def merge_x(at, parts_a, parts_b):
    shapes = [bf16(TOK, 4 * XW)] * 3 + [bf16(TT, 4 * XW)] * 2
    return pl.pallas_call(
        merge_x_kernel,
        in_specs=[SMEM] + vmem_specs(8),
        out_specs=[whole(a) for a in shapes],
        out_shape=shapes,
        compiler_params=params(16),
        cost_estimate=COST,
    )(at, *parts_a, *parts_b)


def local(q_video, k_video, v_video, k_text, v_text, text_len, guide_index, gate, adjoint, w_out):
    h = lax.axis_index("cfg")
    l = lax.axis_index("xlo")
    y = lax.axis_index("y")
    c = lax.axis_index("core")
    z = lax.axis_index("fsdp")
    x = 2 * h + l
    at = jnp.stack([x, y, c]).astype(jnp.int32)

    w_y = jnp.stack([w_out] + [ring_swap(w_out, "y", r) for r in (1, 2, 3)])
    w_z1, w_z3 = ring_swap(w_y, "fsdp", 1), ring_swap(w_y, "fsdp", 3)
    w_parts = [w_y, w_z1, ring_swap(w_z3[:2], "fsdp", 1), ring_swap(w_z1[2:], "fsdp", 3), w_z3]

    own, to1, to3, to2 = cut_x(at, q_video[0], k_video[0], v_video[0], k_text[0, 0], v_text[0, 0])
    got1, got2, got3 = x_swap(to1, 1), x_swap(to2, 2), x_swap(to3, 3)

    guidance = 1.5 + guide_index[0].astype(jnp.float32)
    pass_weight = jnp.where(h == 0, guidance, 1.0 - guidance)
    scaled = (gate[0][None, :] * pass_weight * adjoint[0, 0].astype(jnp.float32)).astype(
        jnp.bfloat16
    )
    scaled, got1, got3 = lax.optimization_barrier((scaled, got1, got3))
    scaled1, scaled3 = x_swap(scaled, 1), x_swap(scaled, 3)
    half = TOK // 2
    adjoints = [scaled, scaled1, x_swap(scaled3[:half], 1), x_swap(scaled1[half:], 3), scaled3]
    messages = cut_y(at, own, got1, got2, got3)
    arrived = [messages[0]] + [ring_swap(messages[r], "y", r) for r in (1, 2, 3)]
    w_z = jnp.concatenate(w_parts, axis=0).reshape(4, *w_y.shape)
    w_z = [lax.dynamic_index_in_dim(w_z, z ^ j, 0, False) for j in range(4)]
    w_own = [jnp.concatenate([part[r] for part in w_z], axis=0) for r in range(4)]
    other = [swap(message, "core") for message in arrived]
    weights = w_own + [swap(piece, "core") for piece in w_own]

    two = jnp.arange(2, dtype=jnp.int32)
    at_core = (c ^ two)[:, None, None, None]
    at_y = (y ^ jnp.arange(4, dtype=jnp.int32))[None, :, None, None]
    at_l = (l ^ two)[None, None, :, None]
    position = ((at_l * 4 + at_y) * 2 + at_core) * TT + jnp.arange(TT, dtype=jnp.int32)
    position = position.reshape(1, -1)
    lens = jnp.where(h == 0, text_len[:, 0], text_len[::-1, 0])
    bias = jnp.where(position < lens[:, None], 0.0, -jnp.inf).astype(jnp.float32)

    to_y = project(at, weights, adjoints)
    dos = [to_y[0]] + [ring_swap(to_y[r], "y", r) for r in (1, 2, 3)]
    other, to_y = lax.optimization_barrier((other, to_y))
    stored = attention_forward(bias, arrived, other)
    dos, stored = lax.optimization_barrier((dos, stored))

    def x_back(parts):
        return [parts[0]] + [x_swap(parts[r], r) for r in (1, 2, 3)]

    def y_back(totals):
        return [totals[0]] + [ring_swap(totals[r], "y", r) for r in (1, 2, 3)]

    dk_sum, dv_sum, dq_0 = attention_backward(stored, dos[:1], False, 0, final=False)
    kept_b, sent_b, dq_b = attention_backward(stored, dos, True)
    totals_b = add_cores(kept_b, swap(sent_b, "core"), dq_b)
    dk_sum, totals_b = lax.optimization_barrier((dk_sum, totals_b))
    got_b = y_back(totals_b)
    kept_a, sent_a, dq_123 = attention_backward(stored, dos[1:], False, 1, (dk_sum, dv_sum))
    sent_a, got_b[1], got_b[3] = lax.optimization_barrier((sent_a, got_b[1], got_b[3]))
    came_a = swap(sent_a, "core")
    came_a, got_b = lax.optimization_barrier((came_a, got_b))
    totals_a = add_cores(kept_a, came_a, dq_0 + dq_123)
    parts_b = x_back(merge_y(at, got_b, True))
    got_a = y_back(totals_a)
    got_a, parts_b = lax.optimization_barrier((got_a, parts_b))
    parts_a = x_back(merge_y(at, got_a, False))
    dq, dk, dv, dkt, dvt = merge_x(at, parts_a, parts_b)
    return dq[None], dk[None], dv[None], dkt[None, None], dvt[None, None]


def solution(mesh):
    devices = mesh.devices
    fine = jax.sharding.Mesh(
        devices.reshape(2, 2, 4, 2, devices.shape[-1]), ("cfg", "xlo", "y", "core", "fsdp")
    )
    seq = ("xlo", "y", "core")
    video = P("fsdp", seq, None)
    per_pass = P("cfg", "fsdp", seq, None)
    placed = (
        video,
        video,
        video,
        per_pass,
        per_pass,
        P(None, "fsdp"),
        P("fsdp"),
        P("fsdp", None),
        per_pass,
        P(("cfg",) + seq + ("fsdp",), None),
    )
    return jax.shard_map(
        local,
        mesh=fine,
        in_specs=placed,
        out_specs=(video, video, video, per_pass, per_pass),
        check_vma=False,
    )
```

```python
import math

import jax
import jax.numpy as jnp
from jax import lax
from jax.experimental import pallas as pl
from jax.experimental.pallas import tpu as pltpu
from jax.sharding import PartitionSpec as P

HD = 128
TOK = 128
TT = 16
XH = 6
XW = XH * HD
WROWS = 96
SCALE = 1.0 / math.sqrt(HD)
EXP2 = SCALE * math.log2(math.e)
VIDK = 2048
TXTK = 256
BLOCK = 256

NT = ((1,), (1,))
NN = ((1,), (0,))
TN = ((0,), (0,))

K_A, V_A, K_B, V_B = 0, 2 * TOK, 4 * TOK, 6 * TOK
TK_A, TV_A, TK_B, TV_B = (8 * TOK + i * 4 * TT for i in range(4))
Q_A = 8 * TOK + 16 * TT
Q_B = Q_A + 2 * TOK
MSG = Q_B + TOK
OWN = 3 * TOK + 2 * TT
NEAR = 3 * TOK // 2 + 2 * TT
BACK_KV = 4 * TOK + 8 * TT


def dot(a, b, dims):
    return lax.dot_general(a, b, (dims, ((), ())), preferred_element_type=jnp.float32)


def vmem_specs(count):
    return [pl.BlockSpec(memory_space=pltpu.VMEM)] * count


SMEM = pl.BlockSpec(memory_space=pltpu.SMEM)
MIB = 1024 * 1024


def params(mib):
    return pltpu.CompilerParams(vmem_limit_bytes=mib * MIB)


COST = pl.CostEstimate(flops=10**6, bytes_accessed=16, transcendentals=0)


def whole(a):
    shape = a.shape
    return pl.BlockSpec(shape, lambda *_: (0,) * len(shape))


def lanes(start, count):
    return pl.ds(pl.multiple_of(start, HD), count)


def swap(a, axis):
    return lax.ppermute(a, axis, [(0, 1), (1, 0)])


def x_swap(a, r):
    if r == 1:
        return swap(a, "xlo")
    if r == 2:
        return swap(a, "cfg")
    return lax.ppermute(a, ("cfg", "xlo"), [(i, 3 - i) for i in range(4)])


def ring_swap(a, axis, r):
    return lax.ppermute(a, axis, [(i, i ^ r) for i in range(4)])


def bf16(*shape):
    return jax.ShapeDtypeStruct(shape, jnp.bfloat16)


def cut_x_kernel(at_ref, *refs):
    del at_ref
    blocks, outs = refs[:17], refs[17:]
    for out, first, count in zip(outs, (0, 5, 10, 15), (5, 5, 5, 2)):
        row = 0
        for block in blocks[first : first + count]:
            out[row : row + block.shape[0]] = block[...]
            row += block.shape[0]


def cut_x(at, q, k, v, kt, vt):
    half = TOK // 2

    def block(rows, r, index):
        return pl.BlockSpec((rows, XW), lambda i, at_ref: (index, at_ref[0] ^ r))

    def same(a):
        return pl.BlockSpec(a.shape, lambda i, at_ref: (0, 0))

    specs, arrays = [], []
    for rows, r, index in ((TOK, 0, 0), (half, 1, 0), (half, 3, 1)):
        specs += [block(rows, r, index)] * 3 + [block(TT, r, 0)] * 2
        arrays += [q, k, v, kt, vt]
    specs += [block(TT, 2, 0)] * 2
    arrays += [kt, vt]
    shapes = [bf16(OWN, XW), bf16(NEAR, XW), bf16(NEAR, XW), bf16(2 * TT, XW)]
    return pl.pallas_call(
        cut_x_kernel,
        grid_spec=pltpu.PrefetchScalarGridSpec(
            num_scalar_prefetch=1,
            grid=(1,),
            in_specs=specs,
            out_specs=[same(a) for a in shapes],
        ),
        out_shape=shapes,
        compiler_params=params(60),
        cost_estimate=COST,
    )(at, *arrays)


def cut_y_kernel(own, got1, got2, got3, outs):
    half = TOK // 2
    quarter = TOK // 4
    for yd in range(4):
        out = outs.at[yd]
        head_a = slice(yd * HD, (yd + 1) * HD)
        head_b = slice((4 + yd // 2) * HD, (5 + yd // 2) * HD)
        for row, tensor, head in (
            (K_A, 1, head_a),
            (V_A, 2, head_a),
            (K_B, 1, head_b),
            (V_B, 2, head_b),
            (Q_A, 0, head_a),
        ):
            out[row : row + TOK] = own[tensor * TOK : (tensor + 1) * TOK, head]
            rows = slice(tensor * half, (tensor + 1) * half)
            out[row + TOK : row + TOK + half] = got1[rows, head]
            out[row + TOK + half : row + 2 * TOK] = got3[rows, head]
        for row, tensor, head in (
            (TK_A, 0, head_a),
            (TV_A, 1, head_a),
            (TK_B, 0, head_b),
            (TV_B, 1, head_b),
        ):
            for s, (src, first) in enumerate(
                ((own, 3 * TOK), (got1, 3 * half), (got2, 0), (got3, 3 * half))
            ):
                start = first + tensor * TT
                out[row + s * TT : row + (s + 1) * TT] = src[start : start + TT, head]
        skip = (yd % 2) * quarter
        for i, (src, first) in enumerate(((own, 0), (own, half), (got1, 0), (got3, 0))):
            rows = slice(first + skip, first + skip + quarter)
            out[Q_B + i * quarter : Q_B + (i + 1) * quarter] = src[rows, head_b]


def cut_y(*arrays):
    shape = bf16(4, MSG, HD)
    return pl.pallas_call(
        cut_y_kernel,
        in_specs=[whole(a) for a in arrays],
        out_specs=whole(shape),
        out_shape=shape,
        compiler_params=params(8),
        cost_estimate=COST,
    )(*arrays)


def project_kernel(at_ref, order, *refs):
    y = at_ref[1]
    w_refs, a_refs, outs = refs[:10], refs[10:15], refs[15:19]
    w_all, a_all, out, sems = refs[19:]
    copies = []
    for refs, whole_ref in ((w_refs, w_all), (a_refs, a_all)):
        row = 0
        for ref in refs:
            copies.append((ref, whole_ref.at[pl.ds(row, ref.shape[0])]))
            row += ref.shape[0]
    started = [pltpu.make_async_copy(src, dst, sems.at[i]) for i, (src, dst) in enumerate(copies)]
    for copy in started:
        copy.start()
    for copy in started:
        copy.wait()
    product = dot(a_all[...], w_all[...], NT).astype(jnp.bfloat16)
    out[...] = dot(product, order[...], NN).astype(jnp.bfloat16)
    quarter = TOK // 4
    for r in range(4):
        yd = y ^ r
        outs[r][: 4 * TOK] = out[:, lanes(yd * HD, HD)]
        head_b = lanes((4 + yd // 2) * HD, HD)
        skip = (yd % 2) * quarter
        for i in range(8):
            rows = pl.ds(pl.multiple_of(i * 2 * quarter + skip, quarter), quarter)
            outs[r][4 * TOK + i * quarter : 4 * TOK + (i + 1) * quarter] = out[rows, head_b]


def project(at, order, weights, adjoints):
    width = weights[0].shape[1]
    rows = 4 * TOK
    return pl.pallas_call(
        project_kernel,
        in_specs=[SMEM, whole(order)] + [pl.BlockSpec(memory_space=pl.ANY)] * 15,
        out_specs=vmem_specs(4),
        out_shape=[bf16(rows + rows // 2, HD)] * 4,
        scratch_shapes=[
            pltpu.VMEM((XW, width), jnp.bfloat16),
            pltpu.VMEM((rows, width), jnp.bfloat16),
            pltpu.VMEM((rows, XW), jnp.bfloat16),
            pltpu.SemaphoreType.DMA((15,)),
        ],
        compiler_params=params(20),
        cost_estimate=COST,
    )(at, order, *weights, *adjoints)


def forward_kernel(at_ref, bias_ref, own, other, *refs):
    e_ref, p_ref, o_ref, w_ref, k_all, v_all, q_ref, q_all = refs
    y = at_ref[1]
    msgs = [ref.at[y ^ r] for ref in (own, other) for r in range(4)]
    step = pl.program_id(0)
    run = 2 * TT

    @pl.when(step == 0)
    def _():
        for head, (k_at, v_at, tk_at, tv_at) in enumerate(
            ((K_A, V_A, TK_A, TV_A), (K_B, V_B, TK_B, TV_B))
        ):
            for i, msg in enumerate(msgs):
                video = slice(i * 2 * TOK, (i + 1) * 2 * TOK)
                k_all[head, video] = msg[k_at : k_at + 2 * TOK]
                v_all[head, video] = msg[v_at : v_at + 2 * TOK]
                for p in range(2):
                    row = VIDK + p * TXTK + i * run
                    k_all[head, row : row + run] = msg[tk_at + p * run : tk_at + (p + 1) * run]
                    v_all[head, row : row + run] = msg[tv_at + p * run : tv_at + (p + 1) * run]
        for r in range(4):
            q_all[r * 2 * TOK : (r + 1) * 2 * TOK] = msgs[r][Q_A : Q_A + 2 * TOK]
            q_all[8 * TOK + r * TOK : 8 * TOK + (r + 1) * TOK] = msgs[r][Q_B : Q_B + TOK]

    head = step // 4
    q = q_all[pl.ds(pl.multiple_of(step * BLOCK, BLOCK), BLOCK)]
    q_ref[...] = q
    s = dot(q, k_all[head, :VIDK], NT)
    mv = jnp.max(s, axis=1, keepdims=True)
    e = jnp.exp2((s - mv) * EXP2)
    lv = jnp.sum(e, axis=1, keepdims=True)
    eb = e.astype(jnp.bfloat16)
    e_ref[...] = eb
    ov = dot(eb, v_all[head, :VIDK], NN)
    o_ref[2] = ov / lv
    for p in range(2):
        text = slice(VIDK + p * TXTK, VIDK + (p + 1) * TXTK)
        st = dot(q, k_all[head, text], NT) + bias_ref[p : p + 1, :]
        m = jnp.maximum(mv, jnp.max(st, axis=1, keepdims=True))
        a = jnp.exp2((mv - m) * EXP2)
        et = jnp.exp2((st - m) * EXP2)
        inv = 1.0 / (a * lv + jnp.sum(et, axis=1, keepdims=True))
        w = a * inv
        pt = (et * inv).astype(jnp.bfloat16)
        p_ref[p] = pt
        w_ref[p] = jnp.broadcast_to(w, w_ref.shape[1:])
        o_ref[p] = w * ov + dot(pt, v_all[head, text], NN)


def attention_forward(at, bias, own, other):
    keys = VIDK + 2 * TXTK
    rows = 12 * TOK
    arrays = (bias, own, other)
    heads = bf16(2, keys, HD)

    def stacked(count, width):
        return pl.BlockSpec((count, BLOCK, width), lambda i: (0, i, 0))

    return pl.pallas_call(
        forward_kernel,
        grid=(rows // BLOCK,),
        in_specs=[SMEM] + [whole(a) for a in arrays],
        out_specs=[
            pl.BlockSpec((BLOCK, VIDK), lambda i: (i, 0)),
            stacked(2, TXTK),
            stacked(3, HD),
            stacked(2, HD),
            whole(heads),
            whole(heads),
            pl.BlockSpec((BLOCK, HD), lambda i: (i, 0)),
        ],
        out_shape=[
            bf16(rows, VIDK),
            bf16(2, rows, TXTK),
            jax.ShapeDtypeStruct((3, rows, HD), jnp.float32),
            jax.ShapeDtypeStruct((2, rows, HD), jnp.float32),
            heads,
            heads,
            bf16(rows, HD),
        ],
        scratch_shapes=[pltpu.VMEM((rows, HD), jnp.bfloat16)],
        compiler_params=params(24),
        cost_estimate=COST,
    )(at, *arrays)


def backward_kernel(shape, *refs):
    parts, first, final, count, do_at = shape
    e_ref, p_ref, o_ref, w_ref, q_ref, k_ref, v_ref = refs[:7]
    dos, refs = refs[7 : 7 + parts], refs[7 + parts :]
    if not first:
        dk_in, dv_in, refs = refs[0], refs[1], refs[2:]
    out0, out1, dqs = refs[0], refs[1], refs[2 : 2 + parts]
    ds_all, dk_acc, dv_acc = refs[2 + parts :]
    step = pl.program_id(0)
    last = pl.num_programs(0) - 1
    per_step = BLOCK // count
    run = 2 * TT

    @pl.when(step == 0)
    def _():
        dk_acc[...] = jnp.zeros_like(dk_acc) if first else dk_in[...]
        dv_acc[...] = jnp.zeros_like(dv_acc) if first else dv_in[...]

    def adjoint(p):
        rows = slice(do_at + p * count, do_at + (p + 1) * count)
        value = jnp.concatenate([ref[rows] for ref in dos[:per_step]], axis=0)
        for i in range(1, parts // per_step):
            group = dos[i * per_step : (i + 1) * per_step]
            other = jnp.concatenate([ref[rows] for ref in group], axis=0)
            value = jnp.where(step == i, other, value)
        return value

    q = q_ref[...]
    v_video = v_ref[:VIDK]
    g = jnp.zeros(q.shape, jnp.float32)
    delta = jnp.zeros((BLOCK, 1), jnp.float32)
    for p in range(2):
        text = slice(VIDK + p * TXTK, VIDK + (p + 1) * TXTK)
        do = adjoint(p)
        do32 = do.astype(jnp.float32)
        w = w_ref[p]
        row_delta = jnp.sum(do32 * o_ref[p], axis=1, keepdims=True)
        g = g + w * do32
        delta = delta + w[:, :1] * row_delta
        pt = p_ref[p]
        ds_text = pt.astype(jnp.float32) * (dot(do, v_ref[text], NT) - row_delta)
        ds_all[:, text] = ds_text.astype(jnp.bfloat16)
        dv_acc[text] += dot(pt, do, TN)
    gb = g.astype(jnp.bfloat16)
    delta = delta + jnp.sum((gb.astype(jnp.float32) - g) * o_ref[2], axis=1, keepdims=True)
    e = e_ref[...]
    ds_video = e.astype(jnp.float32) * (dot(gb, v_video, NT) - delta)
    ds_all[:, :VIDK] = ds_video.astype(jnp.bfloat16)
    dv_acc[:VIDK] += dot(e, gb, TN)
    ds = ds_all[...]
    dk_acc[...] += dot(ds, q, TN)
    dq = (dot(ds, k_ref[...], NN) * SCALE).astype(jnp.bfloat16)
    for r in range(parts):

        @pl.when(step == r // per_step)
        def _():
            start = (r % per_step) * count
            dqs[r][...] = dq[start : start + count]

    @pl.when(step == last)
    def _():
        if not final:
            out0[...] = dk_acc[...]
            out1[...] = dv_acc[...]
            return
        for i in range(8):
            out = (out0, out1)[i // 4].at[i % 4]
            for j, acc, factor in ((0, dk_acc, SCALE), (1, dv_acc, 1.0)):
                video = acc[i * 2 * TOK : (i + 1) * 2 * TOK] * factor
                out[j * 2 * TOK : (j + 1) * 2 * TOK] = video.astype(jnp.bfloat16)
                for p in range(2):
                    src = VIDK + p * TXTK + i * run
                    dst = 4 * TOK + j * 2 * run + p * run
                    out[dst : dst + run] = (acc[src : src + run] * factor).astype(jnp.bfloat16)


def attention_backward(stored, dos, shared, start=0, sums=None, final=True):
    e, p, o, w, k, v, q = stored
    parts = len(dos)
    count = TOK if shared else 2 * TOK
    do_at = 4 * TOK if shared else 0
    steps = parts * count // BLOCK
    head = 1 if shared else 0
    skip = (8 * TOK if shared else 0) // BLOCK + start * count // BLOCK
    keys = VIDK + 2 * TXTK
    shape = (parts, sums is None, final, count, do_at)

    def kernel(*refs):
        backward_kernel(shape, *refs)

    def stacked(depth, width):
        return pl.BlockSpec((depth, BLOCK, width), lambda i: (0, i + skip, 0))

    def rows_of(width):
        return pl.BlockSpec((BLOCK, width), lambda i: (i + skip, 0))

    keys_of = pl.BlockSpec((None, keys, HD), lambda i: (head, 0, 0))
    sum_shape = jax.ShapeDtypeStruct((keys, HD), jnp.float32)
    sums = [] if sums is None else list(sums)
    results = pl.pallas_call(
        kernel,
        grid=(steps,),
        in_specs=[rows_of(VIDK), stacked(2, TXTK), stacked(3, HD), stacked(2, HD), rows_of(HD)]
        + [keys_of, keys_of]
        + vmem_specs(parts + len(sums)),
        out_specs=vmem_specs(2 + parts),
        out_shape=([bf16(4, BACK_KV, HD)] * 2 if final else [sum_shape] * 2)
        + [bf16(count, HD)] * parts,
        scratch_shapes=[
            pltpu.VMEM((BLOCK, keys), jnp.bfloat16),
            pltpu.VMEM((keys, HD), jnp.float32),
            pltpu.VMEM((keys, HD), jnp.float32),
        ],
        compiler_params=params(18),
        cost_estimate=COST,
    )(e, p, o, w, q, k, v, *dos, *sums)
    return results[0], results[1], results[2:]


def add_cores_kernel(kept, came, *refs):
    dqs, outs = refs[:4], refs[4:]
    for r, out in enumerate(outs):
        total = kept[r].astype(jnp.float32) + came[r].astype(jnp.float32)
        out[:BACK_KV] = total.astype(jnp.bfloat16)
        out[BACK_KV:] = dqs[r][...]


def add_cores(kept, came, dqs):
    count = dqs[0].shape[0]
    return pl.pallas_call(
        add_cores_kernel,
        in_specs=vmem_specs(6),
        out_specs=vmem_specs(4),
        out_shape=[bf16(BACK_KV + count, HD)] * 4,
        compiler_params=params(8),
        cost_estimate=COST,
    )(kept, came, *dqs)


def merge_y_kernel(shared, at_ref, *refs):
    y = at_ref[1]
    got, outs = refs[:4], refs[4:]
    quarter = TOK // 4

    def put(out, row, head, value):
        out[row : row + value.shape[0], head] = value

    def part(r, rows):
        if not shared:
            return got[r][rows]
        total = got[r][rows].astype(jnp.float32) + got[r + 1][rows].astype(jnp.float32)
        return total.astype(jnp.bfloat16)

    for r in (0, 2) if shared else range(4):
        head = lanes(((y // 2) ^ (r // 2)) * HD, HD) if shared else lanes((y ^ r) * HD, HD)
        for j in range(2):
            for par in range(2):
                first = (2 * j + par) * TOK
                value = part(r, slice(first, first + TOK))
                for s in (par, par + 2):
                    if (s, par) in ((0, 0), (2, 0), (1, 1), (3, 1)):
                        put(outs[s], (1 + j) * TOK, head, value)
            for s in range(4):
                first = 4 * TOK + j * 4 * TT + s * TT
                value = part(r, slice(first, first + TT))
                put(outs[s], 3 * TOK + j * TT, head, value)
        for par in range(2):
            if not shared:
                value = got[r][BACK_KV + par * TOK : BACK_KV + (par + 1) * TOK]
                for s in (par, par + 2):
                    put(outs[s], 0, head, value)
                continue
            for rr in (r, r + 1):
                skip = ((y ^ rr) % 2) * quarter
                for i in range(2):
                    first = BACK_KV + par * 2 * quarter + i * quarter
                    value = got[rr][first : first + quarter]
                    rows = pl.ds(pl.multiple_of(i * 2 * quarter + skip, quarter), quarter)
                    for s in (par, par + 2):
                        outs[s][rows, head] = value


def merge_y(at, got, shared):
    width = (2 if shared else 4) * HD

    def kernel(*refs):
        merge_y_kernel(shared, *refs)

    return pl.pallas_call(
        kernel,
        in_specs=[SMEM] + vmem_specs(4),
        out_specs=vmem_specs(4),
        out_shape=[bf16(3 * TOK + 2 * TT, width)] * 4,
        compiler_params=params(8),
        cost_estimate=COST,
    )(at, *got)


def merge_x_kernel(at_ref, *refs):
    x = at_ref[0]
    parts_a, parts_b, outs = refs[:4], refs[4:8], refs[8:13]
    for r in range(4):
        for part, first in ((parts_a[r], 0), (parts_b[r], 4 * HD)):
            col = lanes((x ^ r) * XW + first, part.shape[1])
            row = 0
            for out in outs:
                count = out.shape[0]
                out[:, col] = part[row : row + count]
                row += count


def merge_x(at, parts_a, parts_b):
    shapes = [bf16(TOK, 4 * XW)] * 3 + [bf16(TT, 4 * XW)] * 2
    return pl.pallas_call(
        merge_x_kernel,
        in_specs=[SMEM] + vmem_specs(8),
        out_specs=[whole(a) for a in shapes],
        out_shape=shapes,
        compiler_params=params(16),
        cost_estimate=COST,
    )(at, *parts_a, *parts_b)


def local(q_video, k_video, v_video, k_text, v_text, text_len, guide_index, gate, adjoint, w_out):
    h = lax.axis_index("cfg")
    l = lax.axis_index("xlo")
    y = lax.axis_index("y")
    c = lax.axis_index("core")
    z = lax.axis_index("fsdp")
    x = 2 * h + l
    at = jnp.stack([x, y, c]).astype(jnp.int32)

    w_y = [w_out] + [ring_swap(w_out, "y", r) for r in (1, 2, 3)]
    two, four = jnp.arange(2, dtype=jnp.int32), jnp.arange(4, dtype=jnp.int32)
    shard = (y ^ four[None, None, :]) * 2 + (c ^ two[:, None, None])
    shard = shard * 4 + (z ^ four[None, :, None])
    rows = w_out.shape[0]
    channel = shard[..., None] * rows + jnp.arange(rows, dtype=jnp.int32)
    order = channel.reshape(-1, 1) == jnp.arange(XW, dtype=jnp.int32)[None]
    order = order.astype(jnp.bfloat16)

    own, to1, to3, to2 = cut_x(at, q_video[0], k_video[0], v_video[0], k_text[0, 0], v_text[0, 0])
    got1, got2, got3 = x_swap(to1, 1), x_swap(to2, 2), x_swap(to3, 3)
    got2, w_y = lax.optimization_barrier((got2, jnp.concatenate(w_y, axis=0)))
    got1, w_y = lax.optimization_barrier((got1, w_y))
    w_z1, w_z3 = ring_swap(w_y, "fsdp", 1), ring_swap(w_y, "fsdp", 3)
    half = WROWS // 2
    w_z2 = [ring_swap(w_z3[:half], "fsdp", 1), ring_swap(w_z1[half:], "fsdp", 3)]

    guidance = 1.5 + guide_index[0].astype(jnp.float32)
    pass_weight = jnp.where(h == 0, guidance, 1.0 - guidance)
    scaled = (gate[0][None, :] * pass_weight * adjoint[0, 0].astype(jnp.float32)).astype(
        jnp.bfloat16
    )
    scaled, got1, got3 = lax.optimization_barrier((scaled, got1, got3))
    scaled1, scaled3 = x_swap(scaled, 1), x_swap(scaled, 3)
    half = TOK // 2
    adjoints = [scaled, scaled1, x_swap(scaled3[:half], 1), x_swap(scaled1[half:], 3), scaled3]
    messages = cut_y(own, got1, got2, got3)
    arrived = lax.all_to_all(messages, "y", split_axis=0, concat_axis=0, tiled=True)
    w_swapped = [swap(piece, "core") for piece in (w_y, w_z1, w_z3)]
    adjoints, w_z2, w_swapped = lax.optimization_barrier((adjoints, w_z2, w_swapped))
    w_z2_swapped = [swap(piece, "core") for piece in w_z2]
    weights = [w_y, w_z1] + w_z2 + [w_z3] + w_swapped[:2] + w_z2_swapped + w_swapped[2:]
    arrived, weights = lax.optimization_barrier((arrived, weights))
    other = swap(arrived, "core")

    at_core = (c ^ two)[:, None, None, None]
    at_y = (y ^ four)[None, :, None, None]
    at_l = (l ^ two)[None, None, :, None]
    position = ((at_l * 4 + at_y) * 2 + at_core) * TT + jnp.arange(TT, dtype=jnp.int32)
    position = position.reshape(1, -1)
    lens = jnp.where(h == 0, text_len[:, 0], text_len[::-1, 0])
    bias = jnp.where(position < lens[:, None], 0.0, -jnp.inf).astype(jnp.float32)

    to_y = project(at, order, weights, adjoints)
    dos = [to_y[0]] + [ring_swap(to_y[r], "y", r) for r in (1, 2, 3)]
    other, to_y = lax.optimization_barrier((other, to_y))
    stored = attention_forward(at, bias, arrived, other)
    dos, stored = lax.optimization_barrier((dos, stored))

    def x_back(parts):
        return [parts[0]] + [x_swap(parts[r], r) for r in (1, 2, 3)]

    def y_back(totals):
        return [totals[0]] + [ring_swap(totals[r], "y", r) for r in (1, 2, 3)]

    kept_a, sent_a, dq_a = attention_backward(stored, dos, False)
    kept_a, dos = lax.optimization_barrier((kept_a, dos))
    kept_b, sent_b, dq_b = attention_backward(stored, dos, True)
    came_a = swap(sent_a, "core")
    sent_b, came_a = lax.optimization_barrier((sent_b, came_a))
    came_b = swap(sent_b, "core")
    got_a = y_back(add_cores(kept_a, came_a, dq_a))
    total_b = add_cores(kept_b, came_b, dq_b)
    total_b, got_a = lax.optimization_barrier((total_b, got_a))
    parts_a = x_back(merge_y(at, got_a, False))
    got_b = y_back(total_b)
    got_b, parts_a[1], parts_a[2] = lax.optimization_barrier((got_b, parts_a[1], parts_a[2]))
    parts_b = x_back(merge_y(at, got_b, True))
    dq, dk, dv, dkt, dvt = merge_x(at, parts_a, parts_b)
    return dq[None], dk[None], dv[None], dkt[None, None], dvt[None, None]


def solution(mesh):
    devices = mesh.devices
    fine = jax.sharding.Mesh(
        devices.reshape(2, 2, 4, 2, devices.shape[-1]), ("cfg", "xlo", "y", "core", "fsdp")
    )
    seq = ("xlo", "y", "core")
    video = P("fsdp", seq, None)
    per_pass = P("cfg", "fsdp", seq, None)
    placed = (
        video,
        video,
        video,
        per_pass,
        per_pass,
        P(None, "fsdp"),
        P("fsdp"),
        P("fsdp", None),
        per_pass,
        P(("cfg",) + seq + ("fsdp",), None),
    )
    return jax.shard_map(
        local,
        mesh=fine,
        in_specs=placed,
        out_specs=(video, video, video, per_pass, per_pass),
        check_vma=False,
    )
```

```python
import math

import jax
import jax.numpy as jnp
from jax import lax
from jax.experimental import pallas as pl
from jax.experimental.pallas import tpu as pltpu
from jax.sharding import PartitionSpec as P

HD = 128
TOK = 128
TT = 16
XH = 6
XW = XH * HD
WROWS = 96
SCALE = 1.0 / math.sqrt(HD)
EXP2 = SCALE * math.log2(math.e)
VIDK = 2048
TXTK = 256
BLOCK = 512
BACK = 512

NT = ((1,), (1,))
NN = ((1,), (0,))
TN = ((0,), (0,))

K_A, V_A, K_B, V_B = 0, 2 * TOK, 4 * TOK, 6 * TOK
TK_A, TV_A, TK_B, TV_B = (8 * TOK + i * 4 * TT for i in range(4))
Q_A = 8 * TOK + 16 * TT
Q_B = Q_A + 2 * TOK
MSG = Q_B + TOK
OWN = 3 * TOK + 2 * TT
NEAR = 3 * TOK // 2 + 2 * TT
BACK_KV = 4 * TOK + 8 * TT


def dot(a, b, dims):
    return lax.dot_general(a, b, (dims, ((), ())), preferred_element_type=jnp.float32)


def vmem_specs(count):
    return [pl.BlockSpec(memory_space=pltpu.VMEM)] * count


SMEM = pl.BlockSpec(memory_space=pltpu.SMEM)
MIB = 1024 * 1024


def params(mib):
    return pltpu.CompilerParams(vmem_limit_bytes=mib * MIB)


COST = pl.CostEstimate(flops=10**6, bytes_accessed=16, transcendentals=0)


def whole(a):
    shape = a.shape
    return pl.BlockSpec(shape, lambda *_: (0,) * len(shape))


def lanes(start, count):
    return pl.ds(pl.multiple_of(start, HD), count)


def swap(a, axis):
    return lax.ppermute(a, axis, [(0, 1), (1, 0)])


def x_swap(a, r):
    if r == 1:
        return swap(a, "xlo")
    if r == 2:
        return swap(a, "cfg")
    return lax.ppermute(a, ("cfg", "xlo"), [(i, 3 - i) for i in range(4)])


def ring_swap(a, axis, r):
    return lax.ppermute(a, axis, [(i, i ^ r) for i in range(4)])


def bf16(*shape):
    return jax.ShapeDtypeStruct(shape, jnp.bfloat16)


def cut_x_kernel(at_ref, *refs):
    del at_ref
    blocks, outs = refs[:17], refs[17:]
    for out, first, count in zip(outs, (0, 5, 10, 15), (5, 5, 5, 2)):
        row = 0
        for block in blocks[first : first + count]:
            out[row : row + block.shape[0]] = block[...]
            row += block.shape[0]


def cut_x(at, q, k, v, kt, vt):
    half = TOK // 2

    def block(rows, r, index):
        return pl.BlockSpec((rows, XW), lambda i, at_ref: (index, at_ref[0] ^ r))

    def same(a):
        return pl.BlockSpec(a.shape, lambda i, at_ref: (0, 0))

    specs, arrays = [], []
    for rows, r, index in ((TOK, 0, 0), (half, 1, 0), (half, 3, 1)):
        specs += [block(rows, r, index)] * 3 + [block(TT, r, 0)] * 2
        arrays += [q, k, v, kt, vt]
    specs += [block(TT, 2, 0)] * 2
    arrays += [kt, vt]
    shapes = [bf16(OWN, XW), bf16(NEAR, XW), bf16(NEAR, XW), bf16(2 * TT, XW)]
    return pl.pallas_call(
        cut_x_kernel,
        grid_spec=pltpu.PrefetchScalarGridSpec(
            num_scalar_prefetch=1,
            grid=(1,),
            in_specs=specs,
            out_specs=[same(a) for a in shapes],
        ),
        out_shape=shapes,
        compiler_params=params(60),
        cost_estimate=COST,
    )(at, *arrays)


def cut_y_kernel(own, got1, got2, got3, outs):
    half = TOK // 2
    quarter = TOK // 4
    for yd in range(4):
        out = outs.at[yd]
        head_a = slice(yd * HD, (yd + 1) * HD)
        head_b = slice((4 + yd // 2) * HD, (5 + yd // 2) * HD)
        for row, tensor, head in (
            (K_A, 1, head_a),
            (V_A, 2, head_a),
            (K_B, 1, head_b),
            (V_B, 2, head_b),
            (Q_A, 0, head_a),
        ):
            out[row : row + TOK] = own[tensor * TOK : (tensor + 1) * TOK, head]
            rows = slice(tensor * half, (tensor + 1) * half)
            out[row + TOK : row + TOK + half] = got1[rows, head]
            out[row + TOK + half : row + 2 * TOK] = got3[rows, head]
        for row, tensor, head in (
            (TK_A, 0, head_a),
            (TV_A, 1, head_a),
            (TK_B, 0, head_b),
            (TV_B, 1, head_b),
        ):
            for s, (src, first) in enumerate(
                ((own, 3 * TOK), (got1, 3 * half), (got2, 0), (got3, 3 * half))
            ):
                start = first + tensor * TT
                out[row + s * TT : row + (s + 1) * TT] = src[start : start + TT, head]
        skip = (yd % 2) * quarter
        for i, (src, first) in enumerate(((own, 0), (own, half), (got1, 0), (got3, 0))):
            rows = slice(first + skip, first + skip + quarter)
            out[Q_B + i * quarter : Q_B + (i + 1) * quarter] = src[rows, head_b]


def cut_y(*arrays):
    shape = bf16(4, MSG, HD)
    return pl.pallas_call(
        cut_y_kernel,
        in_specs=[whole(a) for a in arrays],
        out_specs=whole(shape),
        out_shape=shape,
        compiler_params=params(8),
        cost_estimate=COST,
    )(*arrays)


def project_kernel(at_ref, order, *refs):
    y = at_ref[1]
    w_refs, a_refs, outs = refs[:10], refs[10:15], refs[15:19]
    w_all, a_all, out, total, sems = refs[19:]
    chunks = sems.shape[0]
    width = w_all.shape[1] // chunks
    started = []
    for j in range(chunks):
        cols = slice(j * width, (j + 1) * width)
        count = 0
        for refs, whole_ref in ((w_refs, w_all), (a_refs, a_all)):
            row = 0
            for ref in refs:
                rows = slice(row, row + ref.shape[0])
                copy = pltpu.make_async_copy(
                    ref.at[:, cols], whole_ref.at[rows, cols], sems.at[j, count]
                )
                copy.start()
                started.append(copy)
                row += ref.shape[0]
                count += 1
    for j in range(chunks):
        cols = slice(j * width, (j + 1) * width)
        for copy in started[j * count : (j + 1) * count]:
            copy.wait()
        term = dot(a_all[:, cols], w_all[:, cols], NT)
        total[...] = term if j == 0 else total[...] + term
    product = total[...].astype(jnp.bfloat16)
    out[...] = dot(product, order[...], NN).astype(jnp.bfloat16)
    quarter = TOK // 4
    for r in range(4):
        yd = y ^ r
        outs[r][: 4 * TOK] = out[:, lanes(yd * HD, HD)]
        head_b = lanes((4 + yd // 2) * HD, HD)
        skip = (yd % 2) * quarter
        for i in range(8):
            rows = pl.ds(pl.multiple_of(i * 2 * quarter + skip, quarter), quarter)
            outs[r][4 * TOK + i * quarter : 4 * TOK + (i + 1) * quarter] = out[rows, head_b]


def project(at, order, weights, adjoints):
    width = weights[0].shape[1]
    rows = 4 * TOK
    return pl.pallas_call(
        project_kernel,
        in_specs=[SMEM, whole(order)] + [pl.BlockSpec(memory_space=pl.ANY)] * 15,
        out_specs=vmem_specs(4),
        out_shape=[bf16(rows + rows // 2, HD)] * 4,
        scratch_shapes=[
            pltpu.VMEM((XW, width), jnp.bfloat16),
            pltpu.VMEM((rows, width), jnp.bfloat16),
            pltpu.VMEM((rows, XW), jnp.bfloat16),
            pltpu.VMEM((rows, XW), jnp.float32),
            pltpu.SemaphoreType.DMA((4, 15)),
        ],
        compiler_params=params(20),
        cost_estimate=COST,
    )(at, order, *weights, *adjoints)


def forward_kernel(at_ref, bias_ref, own, other, *refs):
    e_ref, p_ref, o_ref, w_ref, k_all, v_all, q_ref, q_all = refs
    y = at_ref[1]
    msgs = [ref.at[y ^ r] for ref in (own, other) for r in range(4)]
    step = pl.program_id(0)
    run = 2 * TT

    @pl.when(step == 0)
    def _():
        for head, (k_at, v_at, tk_at, tv_at) in enumerate(
            ((K_A, V_A, TK_A, TV_A), (K_B, V_B, TK_B, TV_B))
        ):
            for i, msg in enumerate(msgs):
                video = slice(i * 2 * TOK, (i + 1) * 2 * TOK)
                k_all[head, video] = msg[k_at : k_at + 2 * TOK]
                v_all[head, video] = msg[v_at : v_at + 2 * TOK]
                for p in range(2):
                    row = VIDK + p * TXTK + i * run
                    k_all[head, row : row + run] = msg[tk_at + p * run : tk_at + (p + 1) * run]
                    v_all[head, row : row + run] = msg[tv_at + p * run : tv_at + (p + 1) * run]
        for r in range(4):
            q_all[r * 2 * TOK : (r + 1) * 2 * TOK] = msgs[r][Q_A : Q_A + 2 * TOK]
            q_all[8 * TOK + r * TOK : 8 * TOK + (r + 1) * TOK] = msgs[r][Q_B : Q_B + TOK]

    head = step * BLOCK // (8 * TOK)
    q = q_all[pl.ds(pl.multiple_of(step * BLOCK, BLOCK), BLOCK)]
    q_ref[...] = q
    s = dot(q, k_all[head, :VIDK], NT)
    mv = jnp.max(s, axis=1, keepdims=True)
    e = jnp.exp2((s - mv) * EXP2)
    lv = jnp.sum(e, axis=1, keepdims=True)
    eb = e.astype(jnp.bfloat16)
    e_ref[...] = eb
    ov = dot(eb, v_all[head, :VIDK], NN)
    o_ref[2] = ov / lv
    for p in range(2):
        text = slice(VIDK + p * TXTK, VIDK + (p + 1) * TXTK)
        st = dot(q, k_all[head, text], NT) + bias_ref[p : p + 1, :]
        m = jnp.maximum(mv, jnp.max(st, axis=1, keepdims=True))
        a = jnp.exp2((mv - m) * EXP2)
        et = jnp.exp2((st - m) * EXP2)
        inv = 1.0 / (a * lv + jnp.sum(et, axis=1, keepdims=True))
        w = a * inv
        pt = (et * inv).astype(jnp.bfloat16)
        p_ref[p] = pt
        w_ref[p] = jnp.broadcast_to(w, w_ref.shape[1:])
        o_ref[p] = w * ov + dot(pt, v_all[head, text], NN)


def attention_forward(at, bias, own, other):
    keys = VIDK + 2 * TXTK
    rows = 12 * TOK
    arrays = (bias, own, other)
    heads = bf16(2, keys, HD)

    def stacked(count, width):
        return pl.BlockSpec((count, BLOCK, width), lambda i: (0, i, 0))

    return pl.pallas_call(
        forward_kernel,
        grid=(rows // BLOCK,),
        in_specs=[SMEM] + [whole(a) for a in arrays],
        out_specs=[
            pl.BlockSpec((BLOCK, VIDK), lambda i: (i, 0)),
            stacked(2, TXTK),
            stacked(3, HD),
            stacked(2, HD),
            whole(heads),
            whole(heads),
            pl.BlockSpec((BLOCK, HD), lambda i: (i, 0)),
        ],
        out_shape=[
            bf16(rows, VIDK),
            bf16(2, rows, TXTK),
            jax.ShapeDtypeStruct((3, rows, HD), jnp.float32),
            jax.ShapeDtypeStruct((2, rows, HD), jnp.float32),
            heads,
            heads,
            bf16(rows, HD),
        ],
        scratch_shapes=[pltpu.VMEM((rows, HD), jnp.bfloat16)],
        compiler_params=params(32),
        cost_estimate=COST,
    )(at, *arrays)


def backward_kernel(shape, *refs):
    parts, first, final, count, do_at = shape
    e_ref, p_ref, o_ref, w_ref, q_ref, k_ref, v_ref = refs[:7]
    dos, refs = refs[7 : 7 + parts], refs[7 + parts :]
    if not first:
        dk_in, dv_in, refs = refs[0], refs[1], refs[2:]
    out0, out1, dqs = refs[0], refs[1], refs[2 : 2 + parts]
    ds_all, dk_acc, dv_acc = refs[2 + parts :]
    step = pl.program_id(0)
    last = pl.num_programs(0) - 1
    per_step = BACK // count
    run = 2 * TT

    @pl.when(step == 0)
    def _():
        dk_acc[...] = jnp.zeros_like(dk_acc) if first else dk_in[...]
        dv_acc[...] = jnp.zeros_like(dv_acc) if first else dv_in[...]

    def adjoint(p):
        rows = slice(do_at + p * count, do_at + (p + 1) * count)
        value = jnp.concatenate([ref[rows] for ref in dos[:per_step]], axis=0)
        for i in range(1, parts // per_step):
            group = dos[i * per_step : (i + 1) * per_step]
            other = jnp.concatenate([ref[rows] for ref in group], axis=0)
            value = jnp.where(step == i, other, value)
        return value

    q = q_ref[...]
    v_video = v_ref[:VIDK]
    g = jnp.zeros(q.shape, jnp.float32)
    delta = jnp.zeros((BACK, 1), jnp.float32)
    for p in range(2):
        text = slice(VIDK + p * TXTK, VIDK + (p + 1) * TXTK)
        do = adjoint(p)
        do32 = do.astype(jnp.float32)
        w = w_ref[p]
        row_delta = jnp.sum(do32 * o_ref[p], axis=1, keepdims=True)
        g = g + w * do32
        delta = delta + w[:, :1] * row_delta
        pt = p_ref[p]
        ds_text = pt.astype(jnp.float32) * (dot(do, v_ref[text], NT) - row_delta)
        ds_all[:, text] = ds_text.astype(jnp.bfloat16)
        dv_acc[:, text] += dot(do, pt, TN)
    gb = g.astype(jnp.bfloat16)
    delta = delta + jnp.sum((gb.astype(jnp.float32) - g) * o_ref[2], axis=1, keepdims=True)
    e = e_ref[...]
    ds_video = e.astype(jnp.float32) * (dot(gb, v_video, NT) - delta)
    ds_all[:, :VIDK] = ds_video.astype(jnp.bfloat16)
    dv_acc[:, :VIDK] += dot(gb, e, TN)
    ds = ds_all[...]
    dk_acc[...] += dot(q, ds, TN)
    dq = (dot(ds, k_ref[...], NN) * SCALE).astype(jnp.bfloat16)
    for r in range(parts):

        @pl.when(step == r // per_step)
        def _():
            start = (r % per_step) * count
            dqs[r][...] = dq[start : start + count]

    @pl.when(step == last)
    def _():
        if not final:
            out0[...] = dk_acc[...]
            out1[...] = dv_acc[...]
            return
        dk = (dk_acc[...] * SCALE).T
        dv = dv_acc[...].T
        for i in range(8):
            out = (out0, out1)[i // 4].at[i % 4]
            for j, acc in ((0, dk), (1, dv)):
                video = acc[i * 2 * TOK : (i + 1) * 2 * TOK]
                out[j * 2 * TOK : (j + 1) * 2 * TOK] = video.astype(jnp.bfloat16)
                for p in range(2):
                    src = VIDK + p * TXTK + i * run
                    dst = 4 * TOK + j * 2 * run + p * run
                    out[dst : dst + run] = acc[src : src + run].astype(jnp.bfloat16)


def attention_backward(stored, dos, shared, start=0, sums=None, final=True):
    e, p, o, w, k, v, q = stored
    parts = len(dos)
    count = TOK if shared else 2 * TOK
    do_at = 4 * TOK if shared else 0
    steps = parts * count // BACK
    head = 1 if shared else 0
    skip = (8 * TOK if shared else 0) // BACK + start * count // BACK
    keys = VIDK + 2 * TXTK
    shape = (parts, sums is None, final, count, do_at)

    def kernel(*refs):
        backward_kernel(shape, *refs)

    def stacked(depth, width):
        return pl.BlockSpec((depth, BACK, width), lambda i: (0, i + skip, 0))

    def rows_of(width):
        return pl.BlockSpec((BACK, width), lambda i: (i + skip, 0))

    keys_of = pl.BlockSpec((None, keys, HD), lambda i: (head, 0, 0))
    sum_shape = jax.ShapeDtypeStruct((keys, HD), jnp.float32)
    sums = [] if sums is None else list(sums)
    results = pl.pallas_call(
        kernel,
        grid=(steps,),
        in_specs=[rows_of(VIDK), stacked(2, TXTK), stacked(3, HD), stacked(2, HD), rows_of(HD)]
        + [keys_of, keys_of]
        + vmem_specs(parts + len(sums)),
        out_specs=vmem_specs(2 + parts),
        out_shape=([bf16(4, BACK_KV, HD)] * 2 if final else [sum_shape] * 2)
        + [bf16(count, HD)] * parts,
        scratch_shapes=[
            pltpu.VMEM((BACK, keys), jnp.bfloat16),
            pltpu.VMEM((HD, keys), jnp.float32),
            pltpu.VMEM((HD, keys), jnp.float32),
        ],
        compiler_params=params(26),
        cost_estimate=COST,
    )(e, p, o, w, q, k, v, *dos, *sums)
    return results[0], results[1], results[2:]


def add_cores_kernel(kept, came, *refs):
    dqs, outs = refs[:4], refs[4:]
    for r, out in enumerate(outs):
        total = kept[r].astype(jnp.float32) + came[r].astype(jnp.float32)
        out[:BACK_KV] = total.astype(jnp.bfloat16)
        out[BACK_KV:] = dqs[r][...]


def add_cores(kept, came, dqs):
    count = dqs[0].shape[0]
    return pl.pallas_call(
        add_cores_kernel,
        in_specs=vmem_specs(6),
        out_specs=vmem_specs(4),
        out_shape=[bf16(BACK_KV + count, HD)] * 4,
        compiler_params=params(8),
        cost_estimate=COST,
    )(kept, came, *dqs)


def merge_y_kernel(shared, at_ref, *refs):
    y = at_ref[1]
    got, outs = refs[:4], refs[4:]
    quarter = TOK // 4

    def put(out, row, head, value):
        out[row : row + value.shape[0], head] = value

    def part(r, rows):
        if not shared:
            return got[r][rows]
        total = got[r][rows].astype(jnp.float32) + got[r + 1][rows].astype(jnp.float32)
        return total.astype(jnp.bfloat16)

    for r in (0, 2) if shared else range(4):
        head = lanes(((y // 2) ^ (r // 2)) * HD, HD) if shared else lanes((y ^ r) * HD, HD)
        for j in range(2):
            for par in range(2):
                first = (2 * j + par) * TOK
                value = part(r, slice(first, first + TOK))
                for s in (par, par + 2):
                    if (s, par) in ((0, 0), (2, 0), (1, 1), (3, 1)):
                        put(outs[s], (1 + j) * TOK, head, value)
            for s in range(4):
                first = 4 * TOK + j * 4 * TT + s * TT
                value = part(r, slice(first, first + TT))
                put(outs[s], 3 * TOK + j * TT, head, value)
        for par in range(2):
            if not shared:
                value = got[r][BACK_KV + par * TOK : BACK_KV + (par + 1) * TOK]
                for s in (par, par + 2):
                    put(outs[s], 0, head, value)
                continue
            for rr in (r, r + 1):
                skip = ((y ^ rr) % 2) * quarter
                for i in range(2):
                    first = BACK_KV + par * 2 * quarter + i * quarter
                    value = got[rr][first : first + quarter]
                    rows = pl.ds(pl.multiple_of(i * 2 * quarter + skip, quarter), quarter)
                    for s in (par, par + 2):
                        outs[s][rows, head] = value


def merge_y(at, got, shared):
    width = (2 if shared else 4) * HD

    def kernel(*refs):
        merge_y_kernel(shared, *refs)

    return pl.pallas_call(
        kernel,
        in_specs=[SMEM] + vmem_specs(4),
        out_specs=vmem_specs(4),
        out_shape=[bf16(3 * TOK + 2 * TT, width)] * 4,
        compiler_params=params(8),
        cost_estimate=COST,
    )(at, *got)


def merge_x_kernel(at_ref, *refs):
    x = at_ref[0]
    parts_a, parts_b, outs = refs[:4], refs[4:8], refs[8:13]
    for r in range(4):
        for part, first in ((parts_a[r], 0), (parts_b[r], 4 * HD)):
            col = lanes((x ^ r) * XW + first, part.shape[1])
            row = 0
            for out in outs:
                count = out.shape[0]
                out[:, col] = part[row : row + count]
                row += count


def merge_x(at, parts_a, parts_b):
    shapes = [bf16(TOK, 4 * XW)] * 3 + [bf16(TT, 4 * XW)] * 2
    return pl.pallas_call(
        merge_x_kernel,
        in_specs=[SMEM] + vmem_specs(8),
        out_specs=[whole(a) for a in shapes],
        out_shape=shapes,
        compiler_params=params(16),
        cost_estimate=COST,
    )(at, *parts_a, *parts_b)


def local(q_video, k_video, v_video, k_text, v_text, text_len, guide_index, gate, adjoint, w_out):
    h = lax.axis_index("cfg")
    l = lax.axis_index("xlo")
    y = lax.axis_index("y")
    c = lax.axis_index("core")
    z = lax.axis_index("fsdp")
    x = 2 * h + l
    at = jnp.stack([x, y, c]).astype(jnp.int32)

    w_y = [w_out] + [ring_swap(w_out, "y", r) for r in (1, 2, 3)]
    two, four = jnp.arange(2, dtype=jnp.int32), jnp.arange(4, dtype=jnp.int32)
    shard = (y ^ four[None, None, :]) * 2 + (c ^ two[:, None, None])
    shard = shard * 4 + (z ^ four[None, :, None])
    rows = w_out.shape[0]
    channel = shard[..., None] * rows + jnp.arange(rows, dtype=jnp.int32)
    order = channel.reshape(-1, 1) == jnp.arange(XW, dtype=jnp.int32)[None]
    order = order.astype(jnp.bfloat16)

    own, to1, to3, to2 = cut_x(at, q_video[0], k_video[0], v_video[0], k_text[0, 0], v_text[0, 0])
    got1, got2, got3 = x_swap(to1, 1), x_swap(to2, 2), x_swap(to3, 3)
    got2, w_y = lax.optimization_barrier((got2, jnp.concatenate(w_y, axis=0)))
    w_y_swapped = swap(w_y, "core")
    got1, w_y_swapped = lax.optimization_barrier((got1, w_y_swapped))
    w_z1, w_z3 = ring_swap(w_y, "fsdp", 1), ring_swap(w_y, "fsdp", 3)
    half = WROWS // 2
    w_z2 = [ring_swap(w_z3[:half], "fsdp", 1), ring_swap(w_z1[half:], "fsdp", 3)]

    guidance = 1.5 + guide_index[0].astype(jnp.float32)
    pass_weight = jnp.where(h == 0, guidance, 1.0 - guidance)
    scaled = (gate[0][None, :] * pass_weight * adjoint[0, 0].astype(jnp.float32)).astype(
        jnp.bfloat16
    )
    scaled, got1, got3 = lax.optimization_barrier((scaled, got1, got3))
    scaled1, scaled3 = x_swap(scaled, 1), x_swap(scaled, 3)
    half = TOK // 2
    adjoints = [scaled, scaled1, x_swap(scaled3[:half], 1), x_swap(scaled1[half:], 3), scaled3]
    messages = cut_y(own, got1, got2, got3)
    arrived = lax.all_to_all(messages, "y", split_axis=0, concat_axis=0, tiled=True)
    w_swapped = [w_y_swapped, swap(w_z1, "core"), swap(w_z3, "core")]
    adjoints, w_z2, w_swapped = lax.optimization_barrier((adjoints, w_z2, w_swapped))
    w_z2_swapped = [swap(piece, "core") for piece in w_z2]
    weights = [w_y, w_z1] + w_z2 + [w_z3] + w_swapped[:2] + w_z2_swapped + w_swapped[2:]
    arrived, weights = lax.optimization_barrier((arrived, weights))
    other = swap(arrived, "core")

    at_core = (c ^ two)[:, None, None, None]
    at_y = (y ^ four)[None, :, None, None]
    at_l = (l ^ two)[None, None, :, None]
    position = ((at_l * 4 + at_y) * 2 + at_core) * TT + jnp.arange(TT, dtype=jnp.int32)
    position = position.reshape(1, -1)
    lens = jnp.where(h == 0, text_len[:, 0], text_len[::-1, 0])
    bias = jnp.where(position < lens[:, None], 0.0, -jnp.inf).astype(jnp.float32)

    to_y = project(at, order, weights, adjoints)
    dos = [to_y[0]] + [ring_swap(to_y[r], "y", r) for r in (1, 2, 3)]
    other, to_y = lax.optimization_barrier((other, to_y))
    stored = attention_forward(at, bias, arrived, other)
    dos, stored = lax.optimization_barrier((dos, stored))

    def x_back(parts):
        return [parts[0]] + [x_swap(parts[r], r) for r in (1, 2, 3)]

    def y_back(totals):
        return [totals[0]] + [ring_swap(totals[r], "y", r) for r in (1, 2, 3)]

    kept_a, sent_a, dq_a = attention_backward(stored, dos, False)
    kept_a, dos = lax.optimization_barrier((kept_a, dos))
    kept_b, sent_b, dq_b = attention_backward(stored, dos, True)
    came_a = swap(sent_a, "core")
    sent_b, came_a = lax.optimization_barrier((sent_b, came_a))
    came_b = swap(sent_b, "core")
    got_a = y_back(add_cores(kept_a, came_a, dq_a))
    total_b = add_cores(kept_b, came_b, dq_b)
    total_b, got_a = lax.optimization_barrier((total_b, got_a))
    parts_a = x_back(merge_y(at, got_a, False))
    got_b = y_back(total_b)
    got_b, parts_a[1] = lax.optimization_barrier((got_b, parts_a[1]))
    parts_b = x_back(merge_y(at, got_b, True))
    dq, dk, dv, dkt, dvt = merge_x(at, parts_a, parts_b)
    return dq[None], dk[None], dv[None], dkt[None, None], dvt[None, None]


def solution(mesh):
    devices = mesh.devices
    fine = jax.sharding.Mesh(
        devices.reshape(2, 2, 4, 2, devices.shape[-1]), ("cfg", "xlo", "y", "core", "fsdp")
    )
    seq = ("xlo", "y", "core")
    video = P("fsdp", seq, None)
    per_pass = P("cfg", "fsdp", seq, None)
    placed = (
        video,
        video,
        video,
        per_pass,
        per_pass,
        P(None, "fsdp"),
        P("fsdp"),
        P("fsdp", None),
        per_pass,
        P(("cfg",) + seq + ("fsdp",), None),
    )
    return jax.shard_map(
        local,
        mesh=fine,
        in_specs=placed,
        out_specs=(video, video, video, per_pass, per_pass),
        check_vma=False,
    )
```

```python
import math

import jax
import jax.numpy as jnp
from jax import lax
from jax.experimental import pallas as pl
from jax.experimental.pallas import tpu as pltpu
from jax.sharding import PartitionSpec as P

HD = 128
TOK = 128
TT = 16
XH = 6
XW = XH * HD
WROWS = 96
SCALE = 1.0 / math.sqrt(HD)
EXP2 = SCALE * math.log2(math.e)
VIDK = 2048
TXTK = 256
BLOCK = 512
BACK = 512

NT = ((1,), (1,))
NN = ((1,), (0,))
TN = ((0,), (0,))

K_A, V_A, K_B, V_B = 0, 2 * TOK, 4 * TOK, 6 * TOK
TK_A, TV_A, TK_B, TV_B = (8 * TOK + i * 4 * TT for i in range(4))
Q_A = 8 * TOK + 16 * TT
Q_B = Q_A + 2 * TOK
MSG = Q_B + TOK
OWN = 3 * TOK + 2 * TT
NEAR = 3 * TOK // 2 + 2 * TT
BACK_KV = 4 * TOK + 8 * TT


def dot(a, b, dims):
    return lax.dot_general(a, b, (dims, ((), ())), preferred_element_type=jnp.float32)


def vmem_specs(count):
    return [pl.BlockSpec(memory_space=pltpu.VMEM)] * count


SMEM = pl.BlockSpec(memory_space=pltpu.SMEM)
MIB = 1024 * 1024


def params(mib):
    return pltpu.CompilerParams(vmem_limit_bytes=mib * MIB)


COST = pl.CostEstimate(flops=10**6, bytes_accessed=16, transcendentals=0)


def whole(a):
    shape = a.shape
    return pl.BlockSpec(shape, lambda *_: (0,) * len(shape))


def lanes(start, count):
    return pl.ds(pl.multiple_of(start, HD), count)


def swap(a, axis):
    return lax.ppermute(a, axis, [(0, 1), (1, 0)])


def x_swap(a, r):
    if r == 1:
        return swap(a, "xlo")
    if r == 2:
        return swap(a, "cfg")
    return lax.ppermute(a, ("cfg", "xlo"), [(i, 3 - i) for i in range(4)])


def ring_swap(a, axis, r):
    return lax.ppermute(a, axis, [(i, i ^ r) for i in range(4)])


def bf16(*shape):
    return jax.ShapeDtypeStruct(shape, jnp.bfloat16)


def cut_x_kernel(at_ref, *refs):
    del at_ref
    blocks, outs = refs[:17], refs[17:]
    for out, first, count in zip(outs, (0, 5, 10, 15), (5, 5, 5, 2)):
        row = 0
        for block in blocks[first : first + count]:
            out[row : row + block.shape[0]] = block[...]
            row += block.shape[0]


def cut_x(at, q, k, v, kt, vt):
    half = TOK // 2

    def block(rows, r, index):
        return pl.BlockSpec((rows, XW), lambda i, at_ref: (index, at_ref[0] ^ r))

    def same(a):
        return pl.BlockSpec(a.shape, lambda i, at_ref: (0, 0))

    specs, arrays = [], []
    for rows, r, index in ((TOK, 0, 0), (half, 1, 0), (half, 3, 1)):
        specs += [block(rows, r, index)] * 3 + [block(TT, r, 0)] * 2
        arrays += [q, k, v, kt, vt]
    specs += [block(TT, 2, 0)] * 2
    arrays += [kt, vt]
    shapes = [bf16(OWN, XW), bf16(NEAR, XW), bf16(NEAR, XW), bf16(2 * TT, XW)]
    return pl.pallas_call(
        cut_x_kernel,
        grid_spec=pltpu.PrefetchScalarGridSpec(
            num_scalar_prefetch=1,
            grid=(1,),
            in_specs=specs,
            out_specs=[same(a) for a in shapes],
        ),
        out_shape=shapes,
        compiler_params=params(60),
        cost_estimate=COST,
    )(at, *arrays)


def cut_y_kernel(own, got1, got2, got3, outs):
    half = TOK // 2
    quarter = TOK // 4
    for yd in range(4):
        out = outs.at[yd]
        head_a = slice(yd * HD, (yd + 1) * HD)
        head_b = slice((4 + yd // 2) * HD, (5 + yd // 2) * HD)
        for row, tensor, head in (
            (K_A, 1, head_a),
            (V_A, 2, head_a),
            (K_B, 1, head_b),
            (V_B, 2, head_b),
            (Q_A, 0, head_a),
        ):
            out[row : row + TOK] = own[tensor * TOK : (tensor + 1) * TOK, head]
            rows = slice(tensor * half, (tensor + 1) * half)
            out[row + TOK : row + TOK + half] = got1[rows, head]
            out[row + TOK + half : row + 2 * TOK] = got3[rows, head]
        for row, tensor, head in (
            (TK_A, 0, head_a),
            (TV_A, 1, head_a),
            (TK_B, 0, head_b),
            (TV_B, 1, head_b),
        ):
            for s, (src, first) in enumerate(
                ((own, 3 * TOK), (got1, 3 * half), (got2, 0), (got3, 3 * half))
            ):
                start = first + tensor * TT
                out[row + s * TT : row + (s + 1) * TT] = src[start : start + TT, head]
        skip = (yd % 2) * quarter
        for i, (src, first) in enumerate(((own, 0), (own, half), (got1, 0), (got3, 0))):
            rows = slice(first + skip, first + skip + quarter)
            out[Q_B + i * quarter : Q_B + (i + 1) * quarter] = src[rows, head_b]


def cut_y(*arrays):
    shape = bf16(4, MSG, HD)
    return pl.pallas_call(
        cut_y_kernel,
        in_specs=[whole(a) for a in arrays],
        out_specs=whole(shape),
        out_shape=shape,
        compiler_params=params(8),
        cost_estimate=COST,
    )(*arrays)


def project_kernel(at_ref, order, *refs):
    y = at_ref[1]
    w_refs, a_refs, outs = refs[:10], refs[10:15], refs[15:19]
    w_all, a_all, out, total, sems = refs[19:]
    chunks = sems.shape[0]
    width = w_all.shape[1] // chunks
    started = []
    for j in range(chunks):
        cols = slice(j * width, (j + 1) * width)
        count = 0
        for refs, whole_ref in ((w_refs, w_all), (a_refs, a_all)):
            row = 0
            for ref in refs:
                rows = slice(row, row + ref.shape[0])
                copy = pltpu.make_async_copy(
                    ref.at[:, cols], whole_ref.at[rows, cols], sems.at[j, count]
                )
                copy.start()
                started.append(copy)
                row += ref.shape[0]
                count += 1
    for j in range(chunks):
        cols = slice(j * width, (j + 1) * width)
        for copy in started[j * count : (j + 1) * count]:
            copy.wait()
        term = dot(a_all[:, cols], w_all[:, cols], NT)
        total[...] = term if j == 0 else total[...] + term
    product = total[...].astype(jnp.bfloat16)
    out[...] = dot(product, order[...], NN).astype(jnp.bfloat16)
    quarter = TOK // 4
    for r in range(4):
        yd = y ^ r
        outs[r][: 4 * TOK] = out[:, lanes(yd * HD, HD)]
        head_b = lanes((4 + yd // 2) * HD, HD)
        skip = (yd % 2) * quarter
        for i in range(8):
            rows = pl.ds(pl.multiple_of(i * 2 * quarter + skip, quarter), quarter)
            outs[r][4 * TOK + i * quarter : 4 * TOK + (i + 1) * quarter] = out[rows, head_b]


def project(at, order, weights, adjoints):
    width = weights[0].shape[1]
    rows = 4 * TOK
    return pl.pallas_call(
        project_kernel,
        in_specs=[SMEM, whole(order)] + [pl.BlockSpec(memory_space=pl.ANY)] * 15,
        out_specs=vmem_specs(4),
        out_shape=[bf16(rows + rows // 2, HD)] * 4,
        scratch_shapes=[
            pltpu.VMEM((XW, width), jnp.bfloat16),
            pltpu.VMEM((rows, width), jnp.bfloat16),
            pltpu.VMEM((rows, XW), jnp.bfloat16),
            pltpu.VMEM((rows, XW), jnp.float32),
            pltpu.SemaphoreType.DMA((4, 15)),
        ],
        compiler_params=params(20),
        cost_estimate=COST,
    )(at, order, *weights, *adjoints)


def forward_kernel(at_ref, bias_ref, own, other, *refs):
    e_ref, p_ref, o_ref, w_ref, k_all, v_all, q_ref, q_all = refs
    y = at_ref[1]
    msgs = [ref.at[y ^ r] for ref in (own, other) for r in range(4)]
    step = pl.program_id(0)
    run = 2 * TT

    @pl.when(step == 0)
    def _():
        for head, (k_at, v_at, tk_at, tv_at) in enumerate(
            ((K_A, V_A, TK_A, TV_A), (K_B, V_B, TK_B, TV_B))
        ):
            for i, msg in enumerate(msgs):
                video = slice(i * 2 * TOK, (i + 1) * 2 * TOK)
                k_all[head, video] = msg[k_at : k_at + 2 * TOK]
                v_all[head, video] = msg[v_at : v_at + 2 * TOK]
                for p in range(2):
                    row = VIDK + p * TXTK + i * run
                    k_all[head, row : row + run] = msg[tk_at + p * run : tk_at + (p + 1) * run]
                    v_all[head, row : row + run] = msg[tv_at + p * run : tv_at + (p + 1) * run]
        for r in range(4):
            q_all[r * 2 * TOK : (r + 1) * 2 * TOK] = msgs[r][Q_A : Q_A + 2 * TOK]
            q_all[8 * TOK + r * TOK : 8 * TOK + (r + 1) * TOK] = msgs[r][Q_B : Q_B + TOK]

    head = step * BLOCK // (8 * TOK)
    q = q_all[pl.ds(pl.multiple_of(step * BLOCK, BLOCK), BLOCK)]
    q_ref[...] = q
    s = dot(q, k_all[head, :VIDK], NT)
    mv = jnp.max(s, axis=1, keepdims=True)
    e = jnp.exp2((s - mv) * EXP2)
    lv = jnp.sum(e, axis=1, keepdims=True)
    eb = e.astype(jnp.bfloat16)
    e_ref[...] = eb
    ov = dot(eb, v_all[head, :VIDK], NN)
    o_ref[2] = ov / lv
    for p in range(2):
        text = slice(VIDK + p * TXTK, VIDK + (p + 1) * TXTK)
        st = dot(q, k_all[head, text], NT) + bias_ref[p : p + 1, :]
        m = jnp.maximum(mv, jnp.max(st, axis=1, keepdims=True))
        a = jnp.exp2((mv - m) * EXP2)
        et = jnp.exp2((st - m) * EXP2)
        inv = 1.0 / (a * lv + jnp.sum(et, axis=1, keepdims=True))
        w = a * inv
        pt = (et * inv).astype(jnp.bfloat16)
        p_ref[p] = pt
        w_ref[p] = jnp.broadcast_to(w, w_ref.shape[1:])
        o_ref[p] = w * ov + dot(pt, v_all[head, text], NN)


def attention_forward(at, bias, own, other):
    keys = VIDK + 2 * TXTK
    rows = 12 * TOK
    arrays = (bias, own, other)
    heads = bf16(2, keys, HD)

    def stacked(count, width):
        return pl.BlockSpec((count, BLOCK, width), lambda i: (0, i, 0))

    return pl.pallas_call(
        forward_kernel,
        grid=(rows // BLOCK,),
        in_specs=[SMEM] + [whole(a) for a in arrays],
        out_specs=[
            pl.BlockSpec((BLOCK, VIDK), lambda i: (i, 0)),
            stacked(2, TXTK),
            stacked(3, HD),
            stacked(2, HD),
            whole(heads),
            whole(heads),
            pl.BlockSpec((BLOCK, HD), lambda i: (i, 0)),
        ],
        out_shape=[
            bf16(rows, VIDK),
            bf16(2, rows, TXTK),
            jax.ShapeDtypeStruct((3, rows, HD), jnp.float32),
            jax.ShapeDtypeStruct((2, rows, HD), jnp.float32),
            heads,
            heads,
            bf16(rows, HD),
        ],
        scratch_shapes=[pltpu.VMEM((rows, HD), jnp.bfloat16)],
        compiler_params=params(32),
        cost_estimate=COST,
    )(at, *arrays)


def backward_kernel(shape, *refs):
    parts, first, final, count, do_at = shape
    e_ref, p_ref, o_ref, w_ref, q_ref, k_ref, v_ref = refs[:7]
    dos, refs = refs[7 : 7 + parts], refs[7 + parts :]
    if not first:
        dk_in, dv_in, refs = refs[0], refs[1], refs[2:]
    out0, out1, dqs = refs[0], refs[1], refs[2 : 2 + parts]
    ds_all, dk_acc, dv_acc = refs[2 + parts :]
    step = pl.program_id(0)
    last = pl.num_programs(0) - 1
    per_step = BACK // count
    run = 2 * TT

    @pl.when(step == 0)
    def _():
        dk_acc[...] = jnp.zeros_like(dk_acc) if first else dk_in[...]
        dv_acc[...] = jnp.zeros_like(dv_acc) if first else dv_in[...]

    def adjoint(p):
        rows = slice(do_at + p * count, do_at + (p + 1) * count)
        value = jnp.concatenate([ref[rows] for ref in dos[:per_step]], axis=0)
        for i in range(1, parts // per_step):
            group = dos[i * per_step : (i + 1) * per_step]
            other = jnp.concatenate([ref[rows] for ref in group], axis=0)
            value = jnp.where(step == i, other, value)
        return value

    q = q_ref[...]
    v_video = v_ref[:VIDK]
    g = jnp.zeros(q.shape, jnp.float32)
    delta = jnp.zeros((BACK, 1), jnp.float32)
    for p in range(2):
        text = slice(VIDK + p * TXTK, VIDK + (p + 1) * TXTK)
        do = adjoint(p)
        do32 = do.astype(jnp.float32)
        w = w_ref[p]
        row_delta = jnp.sum(do32 * o_ref[p], axis=1, keepdims=True)
        g = g + w * do32
        delta = delta + w[:, :1] * row_delta
        pt = p_ref[p]
        ds_text = pt.astype(jnp.float32) * (dot(do, v_ref[text], NT) - row_delta)
        ds_all[:, text] = ds_text.astype(jnp.bfloat16)
        dv_acc[:, text] += dot(do, pt, TN)
    gb = g.astype(jnp.bfloat16)
    delta = delta + jnp.sum((gb.astype(jnp.float32) - g) * o_ref[2], axis=1, keepdims=True)
    e = e_ref[...]
    ds_video = e.astype(jnp.float32) * (dot(gb, v_video, NT) - delta)
    ds_all[:, :VIDK] = ds_video.astype(jnp.bfloat16)
    dv_acc[:, :VIDK] += dot(gb, e, TN)
    ds = ds_all[...]
    dk_acc[...] += dot(q, ds, TN)
    dq = (dot(ds, k_ref[...], NN) * SCALE).astype(jnp.bfloat16)
    for r in range(parts):

        @pl.when(step == r // per_step)
        def _():
            start = (r % per_step) * count
            dqs[r][...] = dq[start : start + count]

    @pl.when(step == last)
    def _():
        if not final:
            out0[...] = dk_acc[...]
            out1[...] = dv_acc[...]
            return
        dk = (dk_acc[...] * SCALE).T
        dv = dv_acc[...].T
        for i in range(8):
            out = (out0, out1)[i // 4].at[i % 4]
            for j, acc in ((0, dk), (1, dv)):
                video = acc[i * 2 * TOK : (i + 1) * 2 * TOK]
                out[j * 2 * TOK : (j + 1) * 2 * TOK] = video.astype(jnp.bfloat16)
                for p in range(2):
                    src = VIDK + p * TXTK + i * run
                    dst = 4 * TOK + j * 2 * run + p * run
                    out[dst : dst + run] = acc[src : src + run].astype(jnp.bfloat16)


def attention_backward(stored, dos, shared, start=0, sums=None, final=True):
    e, p, o, w, k, v, q = stored
    parts = len(dos)
    count = TOK if shared else 2 * TOK
    do_at = 4 * TOK if shared else 0
    steps = parts * count // BACK
    head = 1 if shared else 0
    skip = (8 * TOK if shared else 0) // BACK + start * count // BACK
    keys = VIDK + 2 * TXTK
    shape = (parts, sums is None, final, count, do_at)

    def kernel(*refs):
        backward_kernel(shape, *refs)

    def stacked(depth, width):
        return pl.BlockSpec((depth, BACK, width), lambda i: (0, i + skip, 0))

    def rows_of(width):
        return pl.BlockSpec((BACK, width), lambda i: (i + skip, 0))

    keys_of = pl.BlockSpec((None, keys, HD), lambda i: (head, 0, 0))
    sum_shape = jax.ShapeDtypeStruct((keys, HD), jnp.float32)
    sums = [] if sums is None else list(sums)
    results = pl.pallas_call(
        kernel,
        grid=(steps,),
        in_specs=[rows_of(VIDK), stacked(2, TXTK), stacked(3, HD), stacked(2, HD), rows_of(HD)]
        + [keys_of, keys_of]
        + vmem_specs(parts + len(sums)),
        out_specs=vmem_specs(2 + parts),
        out_shape=([bf16(4, BACK_KV, HD)] * 2 if final else [sum_shape] * 2)
        + [bf16(count, HD)] * parts,
        scratch_shapes=[
            pltpu.VMEM((BACK, keys), jnp.bfloat16),
            pltpu.VMEM((HD, keys), jnp.float32),
            pltpu.VMEM((HD, keys), jnp.float32),
        ],
        compiler_params=params(26),
        cost_estimate=COST,
    )(e, p, o, w, q, k, v, *dos, *sums)
    return results[0], results[1], results[2:]


def add_cores_kernel(kept, came, *refs):
    dqs, outs = refs[:4], refs[4:]
    for r, out in enumerate(outs):
        total = kept[r].astype(jnp.float32) + came[r].astype(jnp.float32)
        out[:BACK_KV] = total.astype(jnp.bfloat16)
        out[BACK_KV:] = dqs[r][...]


def add_cores(kept, came, dqs):
    count = dqs[0].shape[0]
    return pl.pallas_call(
        add_cores_kernel,
        in_specs=vmem_specs(6),
        out_specs=vmem_specs(4),
        out_shape=[bf16(BACK_KV + count, HD)] * 4,
        compiler_params=params(8),
        cost_estimate=COST,
    )(kept, came, *dqs)


def merge_y_kernel(shared, at_ref, *refs):
    y = at_ref[1]
    got, outs = refs[:4], refs[4:]
    quarter = TOK // 4

    def put(out, row, head, value):
        out[row : row + value.shape[0], head] = value

    def part(r, rows):
        if not shared:
            return got[r][rows]
        total = got[r][rows].astype(jnp.float32) + got[r + 1][rows].astype(jnp.float32)
        return total.astype(jnp.bfloat16)

    for r in (0, 2) if shared else range(4):
        head = lanes(((y // 2) ^ (r // 2)) * HD, HD) if shared else lanes((y ^ r) * HD, HD)
        for j in range(2):
            for par in range(2):
                first = (2 * j + par) * TOK
                value = part(r, slice(first, first + TOK))
                for s in (par, par + 2):
                    if (s, par) in ((0, 0), (2, 0), (1, 1), (3, 1)):
                        put(outs[s], (1 + j) * TOK, head, value)
            for s in range(4):
                first = 4 * TOK + j * 4 * TT + s * TT
                value = part(r, slice(first, first + TT))
                put(outs[s], 3 * TOK + j * TT, head, value)
        for par in range(2):
            if not shared:
                value = got[r][BACK_KV + par * TOK : BACK_KV + (par + 1) * TOK]
                for s in (par, par + 2):
                    put(outs[s], 0, head, value)
                continue
            for rr in (r, r + 1):
                skip = ((y ^ rr) % 2) * quarter
                for i in range(2):
                    first = BACK_KV + par * 2 * quarter + i * quarter
                    value = got[rr][first : first + quarter]
                    rows = pl.ds(pl.multiple_of(i * 2 * quarter + skip, quarter), quarter)
                    for s in (par, par + 2):
                        outs[s][rows, head] = value


def merge_y(at, got, shared):
    width = (2 if shared else 4) * HD

    def kernel(*refs):
        merge_y_kernel(shared, *refs)

    return pl.pallas_call(
        kernel,
        in_specs=[SMEM] + vmem_specs(4),
        out_specs=vmem_specs(4),
        out_shape=[bf16(3 * TOK + 2 * TT, width)] * 4,
        compiler_params=params(8),
        cost_estimate=COST,
    )(at, *got)


def merge_x_kernel(at_ref, *refs):
    x = at_ref[0]
    parts, outs = refs[:4], refs[4:]
    for r in range(4):
        col = lanes((x ^ r) * XW, parts[r].shape[1])
        row = 0
        for out in outs:
            count = out.shape[0]
            out[:, col] = parts[r][row : row + count]
            row += count


def add_shared_kernel(at_ref, *refs):
    x = at_ref[0]
    parts, outs, sems = refs[:4], refs[9:14], refs[14]
    started = []
    for r in range(4):
        col = lanes((x ^ r) * XW + 4 * HD, 2 * HD)
        row = 0
        for i, out in enumerate(outs):
            count = out.shape[0]
            src = parts[r].at[pl.ds(row, count)]
            copy = pltpu.make_async_copy(src, out.at[:, col], sems.at[r, i])
            copy.start()
            started.append(copy)
            row += count
    for copy in started:
        copy.wait()


def merge_x(at, parts_a, parts_b):
    shapes = [bf16(TOK, 4 * XW)] * 3 + [bf16(TT, 4 * XW)] * 2
    placed = pl.pallas_call(
        merge_x_kernel,
        in_specs=[SMEM] + vmem_specs(4),
        out_specs=[whole(a) for a in shapes],
        out_shape=shapes,
        compiler_params=params(16),
        cost_estimate=COST,
    )(at, *parts_a)
    return pl.pallas_call(
        add_shared_kernel,
        in_specs=[SMEM] + vmem_specs(4) + [pl.BlockSpec(memory_space=pl.ANY)] * 5,
        out_specs=[pl.BlockSpec(memory_space=pl.ANY)] * 5,
        out_shape=shapes,
        input_output_aliases={5 + i: i for i in range(5)},
        scratch_shapes=[pltpu.SemaphoreType.DMA((4, 5))],
        compiler_params=params(16),
        cost_estimate=COST,
    )(at, *parts_b, *placed)


def local(q_video, k_video, v_video, k_text, v_text, text_len, guide_index, gate, adjoint, w_out):
    h = lax.axis_index("cfg")
    l = lax.axis_index("xlo")
    y = lax.axis_index("y")
    c = lax.axis_index("core")
    z = lax.axis_index("fsdp")
    x = 2 * h + l
    at = jnp.stack([x, y, c]).astype(jnp.int32)

    w_y = [w_out] + [ring_swap(w_out, "y", r) for r in (1, 2, 3)]
    two, four = jnp.arange(2, dtype=jnp.int32), jnp.arange(4, dtype=jnp.int32)
    shard = (y ^ four[None, None, :]) * 2 + (c ^ two[:, None, None])
    shard = shard * 4 + (z ^ four[None, :, None])
    rows = w_out.shape[0]
    channel = shard[..., None] * rows + jnp.arange(rows, dtype=jnp.int32)
    order = channel.reshape(-1, 1) == jnp.arange(XW, dtype=jnp.int32)[None]
    order = order.astype(jnp.bfloat16)

    own, to1, to3, to2 = cut_x(at, q_video[0], k_video[0], v_video[0], k_text[0, 0], v_text[0, 0])
    got1, got2, got3 = x_swap(to1, 1), x_swap(to2, 2), x_swap(to3, 3)
    got2, w_y = lax.optimization_barrier((got2, jnp.concatenate(w_y, axis=0)))
    w_y_swapped = swap(w_y, "core")
    got1, w_y_swapped = lax.optimization_barrier((got1, w_y_swapped))
    w_z1, w_z3 = ring_swap(w_y, "fsdp", 1), ring_swap(w_y, "fsdp", 3)
    half = WROWS // 2
    w_z2 = [ring_swap(w_z3[:half], "fsdp", 1), ring_swap(w_z1[half:], "fsdp", 3)]

    guidance = 1.5 + guide_index[0].astype(jnp.float32)
    pass_weight = jnp.where(h == 0, guidance, 1.0 - guidance)
    scaled = (gate[0][None, :] * pass_weight * adjoint[0, 0].astype(jnp.float32)).astype(
        jnp.bfloat16
    )
    scaled, got1, got3 = lax.optimization_barrier((scaled, got1, got3))
    scaled1, scaled3 = x_swap(scaled, 1), x_swap(scaled, 3)
    half = TOK // 2
    adjoints = [scaled, scaled1, x_swap(scaled3[:half], 1), x_swap(scaled1[half:], 3), scaled3]
    messages = cut_y(own, got1, got2, got3)
    arrived = lax.all_to_all(messages, "y", split_axis=0, concat_axis=0, tiled=True)
    w_z1, w_z2, w_z3 = lax.optimization_barrier((w_z1, w_z2, w_z3))
    w_swapped = [w_y_swapped, swap(w_z1, "core"), swap(w_z3, "core")]
    w_z2_swapped = [swap(piece, "core") for piece in w_z2]
    weights = [w_y, w_z1] + w_z2 + [w_z3] + w_swapped[:2] + w_z2_swapped + w_swapped[2:]
    arrived, adjoints, weights = lax.optimization_barrier((arrived, adjoints, weights))
    other = swap(arrived, "core")

    at_core = (c ^ two)[:, None, None, None]
    at_y = (y ^ four)[None, :, None, None]
    at_l = (l ^ two)[None, None, :, None]
    position = ((at_l * 4 + at_y) * 2 + at_core) * TT + jnp.arange(TT, dtype=jnp.int32)
    position = position.reshape(1, -1)
    lens = jnp.where(h == 0, text_len[:, 0], text_len[::-1, 0])
    bias = jnp.where(position < lens[:, None], 0.0, -jnp.inf).astype(jnp.float32)

    to_y = project(at, order, weights, adjoints)
    dos = [to_y[0]] + [ring_swap(to_y[r], "y", r) for r in (1, 2, 3)]
    other, to_y = lax.optimization_barrier((other, to_y))
    stored = attention_forward(at, bias, arrived, other)
    dos, stored = lax.optimization_barrier((dos, stored))

    def x_back(parts):
        return [parts[0]] + [x_swap(parts[r], r) for r in (1, 2, 3)]

    def y_back(totals):
        return [totals[0]] + [ring_swap(totals[r], "y", r) for r in (1, 2, 3)]

    kept_a, sent_a, dq_a = attention_backward(stored, dos, False)
    kept_a, dos = lax.optimization_barrier((kept_a, dos))
    kept_b, sent_b, dq_b = attention_backward(stored, dos, True)
    came_a = swap(sent_a, "core")
    sent_b, came_a = lax.optimization_barrier((sent_b, came_a))
    came_b = swap(sent_b, "core")
    got_a = y_back(add_cores(kept_a, came_a, dq_a))
    total_b = add_cores(kept_b, came_b, dq_b)
    total_b, got_a = lax.optimization_barrier((total_b, got_a))
    parts_a = x_back(merge_y(at, got_a, False))
    got_b = y_back(total_b)
    got_b, parts_a[1] = lax.optimization_barrier((got_b, parts_a[1]))
    parts_b = x_back(merge_y(at, got_b, True))
    dq, dk, dv, dkt, dvt = merge_x(at, parts_a, parts_b)
    return dq[None], dk[None], dv[None], dkt[None, None], dvt[None, None]


def solution(mesh):
    devices = mesh.devices
    fine = jax.sharding.Mesh(
        devices.reshape(2, 2, 4, 2, devices.shape[-1]), ("cfg", "xlo", "y", "core", "fsdp")
    )
    seq = ("xlo", "y", "core")
    video = P("fsdp", seq, None)
    per_pass = P("cfg", "fsdp", seq, None)
    placed = (
        video,
        video,
        video,
        per_pass,
        per_pass,
        P(None, "fsdp"),
        P("fsdp"),
        P("fsdp", None),
        per_pass,
        P(("cfg",) + seq + ("fsdp",), None),
    )
    return jax.shard_map(
        local,
        mesh=fine,
        in_specs=placed,
        out_specs=(video, video, video, per_pass, per_pass),
        check_vma=False,
    )
```
